32 devices in a mesh: sec: 4 (over y, x), fsdp: 8 (over z, core).
Axes of the slice: x: 2, y: 2, z: 4, core: 2. Of those that a mesh axis runs over, the one named last changes fastest.
Arguments:
- tokens: bfloat16 [8192, 2560], P(('sec', 'fsdp')), may hold values from -36 to 36
- pre_gain: float32 [2560], replicated, may hold values from 0.1 to 1.9
- w_z: bfloat16 [2560, 2560], P('fsdp'), may hold values from -0.125 to 0.125
- w_x: bfloat16 [2560, 2560], P('fsdp'), may hold values from -0.125 to 0.125
- w_bc: bfloat16 [2560, 256], P('fsdp'), may hold values from -0.125 to 0.125
- w_dt: bfloat16 [2560, 40], P('fsdp'), may hold values from -0.125 to 0.125
- conv_weight: float32 [4, 2816], replicated, may hold values from -0.5 to 0.5
- conv_bias: float32 [2816], replicated, may hold values from -0.5 to 0.5
- dt_bias: float32 [40], replicated, may hold values from -9 to -2
- a_log: float32 [40], replicated, may hold values from -8 to 0
- d_skip: float32 [40], replicated, may hold values from 0.5 to 1.5
- norm_gain: float32 [2560], replicated, may hold values from 0.1 to 1.9
Outputs:
- mixed: bfloat16 [8192, 2560], P(('sec', 'fsdp'))
The draws below stay inside these ranges and needn't reach their ends.
All inputs are finite; a program needn't handle non-finite values.
Results may differ from the reference program's by a relative error of at most 0.015.
Values may be sent and summed in bfloat16 or wider, within the bound.
No kernel may reach another device: no remote copies, remote signals or barrier semaphores. Data moves between devices by JAX's collectives and lax.ppermute only.
A program may use at most 384 MiB of HBM per device.

```python
import math
import jax
import jax.numpy as jnp
from jax import lax

D = 2560
HEADS = 40
HEADDIM = 64
NSTATE = 128
SPAN = 256
CONV_WIDTH = 4
INNER = 2560
SEQ = 8192


def head_mixing(key):
    head_order = jax.random.permutation(jax.random.fold_in(key, 11), HEADS)
    jitter = jax.random.uniform(jax.random.fold_in(key, 13), (HEADS,))
    mixing = (head_order.astype(jnp.float32) + jitter) / HEADS
    fast_rate = 0.04
    slow_rate = 0.5 / SEQ
    head_rate = jnp.exp(math.log(fast_rate) * (1.0 - mixing) + math.log(slow_rate) * mixing)
    target_dt = 0.1 * jnp.sqrt(head_rate / fast_rate)
    return (head_rate, target_dt)


def draw_a_log(key, part):
    head_rate, target_dt = head_mixing(key)
    return jnp.log(head_rate / target_dt).astype(jnp.float32)


def draw_dt_bias(key, part):
    head_rate, target_dt = head_mixing(key)
    return jnp.log(jnp.expm1(target_dt)).astype(jnp.float32)


def draw_tokens(key, part):
    row_scale = jnp.exp(jax.random.uniform(jax.random.fold_in(key, 21), (SEQ, 1), minval=math.log(0.3), maxval=math.log(3.0)))
    col_scale = jnp.exp(jax.random.uniform(jax.random.fold_in(key, 22), (1, D), minval=math.log(0.3), maxval=math.log(3.0)))
    base_part = jnp.clip(jax.random.normal(jax.random.fold_in(key, 23), (SEQ, D)), -4.0, 4.0)
    return (base_part * row_scale * col_scale).astype(jnp.bfloat16)


def block_scale(stream_key, extent, cuts, smallest, largest):
    factor_of = 1.0
    for dim, blocks in cuts:
        steps = jax.random.uniform(jax.random.fold_in(jax.random.fold_in(stream_key, 6), dim), (blocks,), jnp.float32, smallest / len(cuts), largest / len(cuts))
        factor_of = factor_of * jnp.repeat(jnp.exp(steps), extent[dim] // blocks).reshape((-1,) + (1,) * (len(extent) - 1 - dim))
    return factor_of


def bell_draw(own_key, shape, deviation, bound, split=(), kind=jnp.bfloat16):
    level = block_scale(own_key, shape, split, -0.22, 0.18) if split else 1.0
    result = jax.random.normal(own_key, shape, jnp.float32) * deviation * level
    return jnp.minimum(jnp.maximum(result, -bound), bound).astype(kind)


def setup_inputs(seed: int = 0) -> dict:
    streams_of = jax.random.split(jax.random.key(seed), 13)
    return {
        "tokens": draw_tokens(jax.random.fold_in(streams_of[12], 71), 0),
        "pre_gain": jnp.clip(1.0 + 0.18 * jax.random.normal(streams_of[1], (D,), jnp.float32), 0.1, 1.9),
        "w_z": bell_draw(streams_of[2], (D, INNER), D ** -0.5, 0.125, ((0, 8),)),
        "w_x": bell_draw(streams_of[3], (D, INNER), D ** -0.5, 0.125, ((0, 8),)),
        "w_bc": bell_draw(streams_of[4], (D, 2 * NSTATE), D ** -0.5, 0.125, ((0, 8),)),
        "w_dt": bell_draw(streams_of[5], (D, HEADS), D ** -0.5, 0.125, ((0, 8),)),
        "conv_weight": jnp.clip(jax.random.uniform(streams_of[6], (CONV_WIDTH, INNER + 2 * NSTATE), jnp.float32, -0.5, 0.5), -0.5, 0.5),
        "conv_bias": jnp.clip(jax.random.uniform(streams_of[7], (INNER + 2 * NSTATE,), jnp.float32, -0.5, 0.5), -0.5, 0.5),
        "dt_bias": draw_dt_bias(jax.random.fold_in(streams_of[12], 71), 0),
        "a_log": draw_a_log(jax.random.fold_in(streams_of[12], 71), 0),
        "d_skip": jnp.clip(jax.random.uniform(streams_of[10], (HEADS,), jnp.float32, 0.5, 1.5), 0.5, 1.5),
        "norm_gain": jnp.clip(1.0 + 0.18 * jax.random.normal(streams_of[11], (INNER,), jnp.float32), 0.1, 1.9),
    }


EPS = 1e-05

def rms_scale(values, gain_vec):
    mean_square = lax.optimization_barrier(jnp.mean(values * values, axis=-1, keepdims=True))
    return values * lax.rsqrt(mean_square + EPS) * gain_vec

def causal_conv(stacked, kernel, offset_bias):
    kernel_len = kernel.shape[0]
    length = stacked.shape[0] - kernel_len + 1
    summed = offset_bias[None, :]
    for offset in range(kernel_len):
        summed = summed + kernel[offset][None, :] * stacked[offset:offset + length].astype(jnp.float32)
    return jax.nn.silu(summed).astype(jnp.bfloat16)

def block_terms(x_conv, b_conv, c_conv, step_dt, head_rates):
    length = step_dt.shape[1]
    cumulative = jnp.cumsum(step_dt * head_rates, axis=1)
    cum_heads = jnp.swapaxes(cumulative, 1, 2)
    dt_heads = jnp.swapaxes(step_dt, 1, 2)
    inner_dots = jnp.einsum('kqn,ksn->kqs', c_conv.astype(jnp.float32), b_conv.astype(jnp.float32), precision=lax.Precision.HIGHEST)
    causal = lax.broadcasted_iota(jnp.int32, (length, length), 0) >= lax.broadcasted_iota(jnp.int32, (length, length), 1)
    cum_gap = cum_heads[:, :, :, None] - cum_heads[:, :, None, :]
    decays = jnp.where(causal, jnp.exp(-jnp.where(causal, cum_gap, 0.0)), 0.0)
    scores = (decays * dt_heads[:, :, None, :] * inner_dots[:, None, :, :]).astype(jnp.bfloat16)
    y_intra = jnp.einsum('khqs,kshp->kqhp', scores.astype(jnp.float32), x_conv.astype(jnp.float32), precision=lax.Precision.HIGHEST)
    to_end = jnp.exp(-(cumulative[:, -1:, :] - cumulative)) * step_dt
    weighted = (x_conv.astype(jnp.float32) * to_end[..., None]).astype(jnp.bfloat16)
    block_state = jnp.einsum('kshp,ksn->khpn', weighted.astype(jnp.float32), b_conv.astype(jnp.float32), precision=lax.Precision.HIGHEST)
    return (y_intra, block_state, cumulative)

def state_output(c_conv, starts, cumulative):
    reached = jnp.einsum('kqn,khpn->kqhp', c_conv.astype(jnp.float32), starts, precision=lax.Precision.HIGHEST)
    return reached * jnp.exp(-cumulative)[..., None]

def reference(tokens, pre_gain, w_z, w_x, w_bc, w_dt, conv_weight, conv_bias, dt_bias, a_log, d_skip, norm_gain):
    normed = rms_scale(tokens.astype(jnp.float32), pre_gain).astype(jnp.bfloat16)
    grouped = normed.reshape(SEQ // SPAN, SPAN, D)

    def project(row_block):
        return tuple((jnp.dot(row_block, matrix, preferred_element_type=jnp.float32).astype(jnp.bfloat16) for matrix in (w_z, w_x, w_bc, w_dt)))
    z_part, x_part, bc_part, dt_raw = lax.map(project, grouped)
    z_part = z_part.reshape(SEQ, INNER)
    x_part = x_part.reshape(SEQ, INNER)
    bc_part = bc_part.reshape(SEQ, 2 * NSTATE)
    dt_raw = dt_raw.reshape(SEQ, HEADS)
    margin = CONV_WIDTH - 1
    x_conv = causal_conv(jnp.concatenate([jnp.zeros((margin, INNER), jnp.bfloat16), x_part], 0), conv_weight[:, :INNER], conv_bias[:INNER])
    bc_conv = causal_conv(jnp.concatenate([jnp.zeros((margin, 2 * NSTATE), jnp.bfloat16), bc_part], 0), conv_weight[:, INNER:], conv_bias[INNER:])
    step_dt = jax.nn.softplus(dt_raw.astype(jnp.float32) + dt_bias)
    head_rates = jnp.exp(a_log)
    blocks = SEQ // SPAN
    x_blocks = x_conv.reshape(blocks, SPAN, HEADS, HEADDIM)
    b_blocks = bc_conv[:, :NSTATE].reshape(blocks, SPAN, NSTATE)
    c_blocks = bc_conv[:, NSTATE:].reshape(blocks, SPAN, NSTATE)
    dt_blocks = step_dt.reshape(blocks, SPAN, HEADS)

    def span_step(carried, pieces):
        x_one, b_one, c_one, dt_one = pieces
        y_intra, block_state, cumulative = block_terms(x_one[None], b_one[None], c_one[None], dt_one[None], head_rates)
        y_state = state_output(c_one[None], carried[None], cumulative)
        new_state = carried * jnp.exp(-cumulative[0, -1, :])[:, None, None] + block_state[0]
        return (new_state, (y_intra + y_state)[0])
    initial = jnp.zeros((HEADS, HEADDIM, NSTATE), jnp.float32)
    final_state, y_blocks = lax.scan(span_step, initial, (x_blocks, b_blocks, c_blocks, dt_blocks))
    y_total = y_blocks.reshape(SEQ, INNER) + jnp.repeat(d_skip, HEADDIM)[None, :] * x_conv.astype(jnp.float32)
    gated = y_total * jax.nn.silu(z_part.astype(jnp.float32))
    return rms_scale(gated, norm_gain).astype(jnp.bfloat16)
```

```python
import functools
import jax
import jax.numpy as jnp
from jax import lax
from jax.experimental import pallas as pl
from jax.experimental.pallas import tpu as pltpu
from jax.sharding import Mesh, PartitionSpec as P

HEADDIM = 64
EPS = 1e-05
HALO = 16
LANES = 128
VMEM_LIMIT = 48 * 1024 * 1024
ALL = ("sec", "zed", "core")


def params():
    return pltpu.CompilerParams(vmem_limit_bytes=VMEM_LIMIT)


def swapped(value, axis, mask):
    count = lax.axis_size(axis)
    return lax.ppermute(value, axis, [(i, i ^ mask) for i in range(count)])


def following(value):
    count = lax.axis_size(ALL)
    return lax.ppermute(value, ALL, [(i, i + 1) for i in range(count - 1)])


def rms_scale(values, gain_vec):
    mean_square = jnp.mean(values * values, axis=-1, keepdims=True)
    return values * lax.rsqrt(mean_square + EPS) * gain_vec


def spread(columns, first, heads):
    rows = columns.shape[0]
    return jnp.concatenate(
        [
            jnp.broadcast_to(columns[:, first + h : first + h + 1], (rows, HEADDIM))
            for h in range(heads)
        ],
        axis=1,
    )


def block_kernel(heads, state, pre_ref, taps_ref, bias_ref, dtb_ref, rate_ref, skip_ref,
                 y_ref, c_ref, cum_ref, st_ref, wide):
    span = y_ref.shape[0]
    inner = heads * HEADDIM
    conv_width = 2 * state + inner
    taps = taps_ref.shape[0]
    wide[...] = pre_ref[:, :conv_width].astype(jnp.float32)
    acc = bias_ref[...]
    for k in range(taps):
        acc = acc + taps_ref[k : k + 1, :] * wide[pl.ds(HALO - taps + 1 + k, span), :]
    conv = (acc * jax.nn.sigmoid(acc)).astype(jnp.bfloat16)
    b = conv[:, :state]
    c = conv[:, state : 2 * state]
    x = conv[:, 2 * state :]
    c_ref[...] = c
    raw = pre_ref[HALO:, conv_width:].astype(jnp.float32)
    dt = jax.nn.softplus(raw + dtb_ref[...])
    row = lax.broadcasted_iota(jnp.int32, (span, span), 0)
    col = lax.broadcasted_iota(jnp.int32, (span, span), 1)
    causal = row >= col
    cum = jnp.dot(
        causal.astype(jnp.float32),
        dt * rate_ref[...],
        preferred_element_type=jnp.float32,
        precision=lax.Precision.HIGHEST,
    )
    cum_ref[...] = cum
    cum_t = cum.T
    dt_t = dt.T
    inner_dots = lax.dot_general(
        c, b, (((1,), (1,)), ((), ())), preferred_element_type=jnp.float32
    )
    inner_dots = jnp.where(causal, inner_dots, 0.0)
    parts = []
    for h in range(heads):
        gap = cum_t[h : h + 1, :] - cum[:, h : h + 1]
        scores = inner_dots * jnp.exp(jnp.minimum(gap, 0.0)) * dt_t[h : h + 1, :]
        parts.append(
            jnp.dot(
                scores.astype(jnp.bfloat16),
                x[:, h * HEADDIM : (h + 1) * HEADDIM],
                preferred_element_type=jnp.float32,
            )
        )
    x32 = x.astype(jnp.float32)
    y_ref[...] = jnp.concatenate(parts, axis=1) + skip_ref[...] * x32
    to_end = jnp.exp(cum - cum[span - 1 : span, :]) * dt
    weighted = (x32 * spread(to_end, 0, heads)).astype(jnp.bfloat16)
    st_ref[...] = lax.dot_general(
        b, weighted, (((0,), (0,)), ((), ())), preferred_element_type=jnp.float32
    )


def block_call(pre, taps, bias, dtb, rate, skip, heads, state, span):
    inner = heads * HEADDIM
    conv_width = 2 * state + inner
    return pl.pallas_call(
        functools.partial(block_kernel, heads, state),
        out_shape=(
            jax.ShapeDtypeStruct((span, inner), jnp.float32),
            jax.ShapeDtypeStruct((span, state), jnp.bfloat16),
            jax.ShapeDtypeStruct((span, heads), jnp.float32),
            jax.ShapeDtypeStruct((state, inner), jnp.float32),
        ),
        scratch_shapes=[pltpu.VMEM((span + HALO, conv_width), jnp.float32)],
        compiler_params=params(),
    )(pre, taps, bias, dtb, rate, skip)


def pair_kernel(heads, place_ref, st_a, st_b, cum_a, cum_b, pair_ref, decay_ref):
    span = cum_a.shape[0]
    end_a = jnp.exp(-spread(cum_a[span - 1 : span, :], 0, heads))
    end_b = jnp.exp(-spread(cum_b[span - 1 : span, :], 0, heads))
    a_first = place_ref[0] == 0
    scale_a = jnp.where(a_first, end_b, 1.0)
    scale_b = jnp.where(a_first, 1.0, end_a)
    pair_ref[...] = (st_a[...] * scale_a + st_b[...] * scale_b).astype(jnp.bfloat16)
    decay_ref[...] = jnp.broadcast_to(end_a * end_b, decay_ref.shape)


def scan_kernel(sections, depth, place_ref, pair_ref, decay_ref, enter_ref):
    q = place_ref[1]
    z = place_ref[2]
    state, inner = enter_ref.shape[1:]

    def step(k, running):
        s = k // depth
        zz = k % depth
        m = s ^ q

        @pl.when(zz == z)
        def _():
            enter_ref[m] = running

        decay = decay_ref[zz, m][0:1, :]
        return running * decay + pair_ref[zz, m].astype(jnp.float32)

    lax.fori_loop(0, sections * depth, step, jnp.zeros((state, inner), jnp.float32))


def gate_kernel(heads, place_ref, y_a, y_b, c_a, c_b, cum_a, cum_b, st_a, st_b, z_a, z_b,
                enter_ref, out_a, out_b):
    span = y_a.shape[0]
    a_first = place_ref[0] == 0
    enter = enter_ref[...]
    end_a = jnp.exp(-spread(cum_a[span - 1 : span, :], 0, heads))
    end_b = jnp.exp(-spread(cum_b[span - 1 : span, :], 0, heads))
    in_a = jnp.where(a_first, enter, enter * end_b + st_b[...])
    in_b = jnp.where(a_first, enter * end_a + st_a[...], enter)
    for y, c, cum, z, start, out in (
        (y_a, c_a, cum_a, z_a, in_a, out_a),
        (y_b, c_b, cum_b, z_b, in_b, out_b),
    ):
        reached = jnp.dot(
            c[...], start.astype(jnp.bfloat16), preferred_element_type=jnp.float32
        )
        total = y[...] + reached * spread(jnp.exp(-cum[...]), 0, heads)
        gate = z[HALO:, :].astype(jnp.float32)
        out[...] = (total * gate * jax.nn.sigmoid(gate)).astype(jnp.bfloat16)


def norm_kernel(place_ref, own_ref, x_ref, y_ref, d_ref, gain_ref, out_ref):
    q = place_ref[1]
    refs = (own_ref, x_ref, y_ref, d_ref)
    part = own_ref.shape[1]
    sections = len(refs)
    values = [r[...].astype(jnp.float32) for r in refs]
    total = sum(jnp.sum(v * v, axis=-1, keepdims=True) for v in values)
    scale = lax.rsqrt(total / (part * sections) + EPS)
    for s in range(sections):

        @pl.when(q == s)
        def _(s=s):
            for m in range(sections):
                first = (s ^ m) * part
                out_ref[:, first : first + part] = (
                    values[m] * scale * gain_ref[:, first : first + part]
                ).astype(jnp.bfloat16)


def per_device(
    tokens,
    pre_gain,
    w_z,
    w_x,
    w_bc,
    w_dt,
    conv_weight,
    conv_bias,
    dt_bias,
    a_log,
    d_skip,
    norm_gain,
):
    sections, depth, cores = (lax.axis_size(axis) for axis in ALL)
    q, z, c = (lax.axis_index(axis) for axis in ALL)
    span, width = tokens.shape
    state = w_bc.shape[1] // 2
    heads = a_log.shape[0] // (sections * cores)
    inner = heads * HEADDIM
    group = q * cores + c
    place = jnp.stack([c, q, z]).astype(jnp.int32)
    smem = pl.BlockSpec(memory_space=pltpu.SMEM)
    vmem = pl.BlockSpec(memory_space=pltpu.VMEM)

    before = following(tokens[span - HALO :])
    normed = rms_scale(tokens.astype(jnp.float32), pre_gain).astype(jnp.bfloat16)
    halo = rms_scale(before.astype(jnp.float32), pre_gain).astype(jnp.bfloat16)
    own = jnp.concatenate([halo, normed], 0)
    half = own.shape[0] // 2
    from_x = swapped(own, "sec", 1)
    from_y = swapped(own, "sec", 2)
    from_d = jnp.concatenate(
        [swapped(from_y[:half], "sec", 1), swapped(from_x[half:], "sec", 2)], 0
    )
    chunks = [(v, swapped(v, "core", 1)) for v in (own, from_x, from_y, from_d)]

    def columns(matrix):
        mine = lax.dynamic_slice_in_dim(matrix, q * (cores * inner), cores * inner, 1)
        both = lax.all_to_all(mine, "core", split_axis=1, concat_axis=0, tiled=True)
        return lax.all_gather(both, "zed", axis=0, tiled=True)

    small = jnp.concatenate([w_bc, w_dt], 1)
    share = small.shape[0] // sections
    small = lax.dynamic_slice_in_dim(small, q * share, share, 0)
    small = lax.all_gather(small, ALL, axis=0)
    small = small.reshape(sections, depth * cores, share, -1).swapaxes(0, 1)
    small = small.reshape(width, -1)
    full_x = columns(w_x)
    full_z = columns(w_z)
    first = group * heads
    full_dt = lax.dynamic_slice_in_dim(small, 2 * state + first, heads, 1)
    full_pre = jnp.concatenate([small[:, : 2 * state], full_x, full_dt], 1)

    def mine(vector):
        return lax.dynamic_slice_in_dim(vector, first, heads, 0)[None, :]

    def channels(matrix):
        x_side = lax.dynamic_slice_in_dim(matrix, group * inner, inner, 1)
        return jnp.concatenate([matrix[:, -2 * state :], x_side], 1)

    taps = channels(conv_weight)
    bias = channels(conv_bias[None, :])
    dtb = mine(dt_bias)
    rate = jnp.exp(mine(a_log))
    skip = jnp.repeat(mine(d_skip), HEADDIM, axis=1)

    blocks = []
    pairs = []
    decays = []
    for pair_rows in chunks:
        terms = []
        for rows in pair_rows:
            pre = jnp.dot(rows, full_pre, preferred_element_type=jnp.float32)
            terms.append(
                block_call(
                    pre.astype(jnp.bfloat16), taps, bias, dtb, rate, skip, heads, state, span
                )
            )
        (y_a, c_a, cum_a, st_a), (y_b, c_b, cum_b, st_b) = terms
        blocks.append(terms)
        pair, decay = pl.pallas_call(
            functools.partial(pair_kernel, heads),
            out_shape=(
                jax.ShapeDtypeStruct((state, inner), jnp.bfloat16),
                jax.ShapeDtypeStruct((8, inner), jnp.float32),
            ),
            in_specs=[smem] + [vmem] * 4,
            compiler_params=params(),
        )(place, st_a, st_b, cum_a, cum_b)
        pairs.append(pair)
        decays.append(decay)
    all_pairs = lax.all_gather(jnp.stack(pairs), "zed", axis=0)
    all_decays = lax.all_gather(jnp.stack(decays), "zed", axis=0)
    enter = pl.pallas_call(
        functools.partial(scan_kernel, sections, depth),
        out_shape=jax.ShapeDtypeStruct((sections, state, inner), jnp.float32),
        in_specs=[smem, vmem, vmem],
        compiler_params=params(),
    )(place, all_pairs, all_decays)

    gated_a = []
    gated_b = []
    for m, (pair_rows, terms) in enumerate(zip(chunks, blocks)):
        z_a, z_b = (
            jnp.dot(rows, full_z, preferred_element_type=jnp.float32).astype(jnp.bfloat16)
            for rows in pair_rows
        )
        (y_a, c_a, cum_a, st_a), (y_b, c_b, cum_b, st_b) = terms
        out_a, out_b = pl.pallas_call(
            functools.partial(gate_kernel, heads),
            out_shape=(jax.ShapeDtypeStruct((span, inner), jnp.bfloat16),) * 2,
            in_specs=[smem] + [vmem] * 11,
            compiler_params=params(),
        )(place, y_a, y_b, c_a, c_b, cum_a, cum_b, st_a, st_b, z_a, z_b, enter[m])
        gated_a.append(out_a)
        gated_b.append(out_b)
    theirs = swapped(jnp.stack(gated_b), "core", 1)
    pieces = []
    for m in range(sections):
        low = jnp.where(c == 0, gated_a[m], theirs[m])
        high = jnp.where(c == 0, theirs[m], gated_a[m])
        piece = jnp.concatenate([low, high], 1)
        pieces.append(piece if m == 0 else swapped(piece, "sec", m))
    return pl.pallas_call(
        norm_kernel,
        out_shape=jax.ShapeDtypeStruct((span, sections * cores * inner), jnp.bfloat16),
        in_specs=[smem] + [vmem] * 5,
        compiler_params=params(),
    )(place, *pieces, norm_gain[None, :])


def solution(mesh):
    sections, fsdp = (mesh.shape[axis] for axis in ("sec", "fsdp"))
    split = Mesh(mesh.devices.reshape(sections, fsdp // 2, 2), ALL)
    rows = P(("zed", "core"), None)
    placed = (P(ALL, None), P(), rows, rows, rows, rows, P(), P(), P(), P(), P(), P())
    return jax.shard_map(
        per_device, mesh=split, in_specs=placed, out_specs=P(ALL, None), check_vma=False
    )
```

```python
import functools
import jax
import jax.numpy as jnp
from jax import lax
from jax.experimental import pallas as pl
from jax.experimental.pallas import tpu as pltpu
from jax.sharding import Mesh, PartitionSpec as P

HEADDIM = 64
EPS = 1e-05
HALO = 16
LANES = 128
VMEM_LIMIT = 48 * 1024 * 1024
ALL = ("sec", "zed", "core")


def params():
    return pltpu.CompilerParams(vmem_limit_bytes=VMEM_LIMIT)


def swapped(value, axis, mask):
    count = lax.axis_size(axis)
    return lax.ppermute(value, axis, [(i, i ^ mask) for i in range(count)])


def routed(value, masks):
    sections, depth, cores = (lax.axis_size(axis) for axis in ALL)
    pairs = []
    for s in range(sections):
        for z in range(depth):
            for c in range(cores):
                place = z * cores + c
                pairs.append(
                    (s * depth * cores + place, (s ^ masks[c]) * depth * cores + place)
                )
    return lax.ppermute(value, ALL, pairs)


def following(value):
    count = lax.axis_size(ALL)
    return lax.ppermute(value, ALL, [(i, i + 1) for i in range(count - 1)])


def line_gather(value, axis):
    count = lax.axis_size(axis)
    up, down = [value], [value]
    for r in range(1, count):
        up.append(lax.ppermute(up[-1], axis, [(i, i + 1) for i in range(r - 1, count - 1)]))
        down.append(lax.ppermute(down[-1], axis, [(i, i - 1) for i in range(1, count - r + 1)]))
    return up, down


def placed_line(up, down, axis):
    count, mine = lax.axis_size(axis), lax.axis_index(axis)
    out = jnp.zeros((count,) + up[0].shape, up[0].dtype)
    zeros = (0,) * up[0].ndim
    for r in range(count):
        block = up[0] if r == 0 else jnp.where(mine >= r, up[r], down[count - r])
        out = lax.dynamic_update_slice(out, block[None], ((mine - r) % count,) + zeros)
    return out


def rms_scale(values, gain_vec):
    mean_square = jnp.mean(values * values, axis=-1, keepdims=True)
    return values * lax.rsqrt(mean_square + EPS) * gain_vec


def spread(columns, heads):
    rows = columns.shape[0]
    return jnp.concatenate(
        [jnp.broadcast_to(columns[:, h : h + 1], (rows, HEADDIM)) for h in range(heads)],
        axis=1,
    )


def block_kernel(heads, state, rows_ref, mat_ref, taps_ref, bias_ref, dtb_ref, rate_ref,
                 skip_ref, y_ref, c_ref, cum_ref, st_ref, wide):
    span = y_ref.shape[0]
    inner = heads * HEADDIM
    conv_width = 2 * state + inner
    taps = taps_ref.shape[0]
    pre = jnp.dot(rows_ref[...], mat_ref[...], preferred_element_type=jnp.float32)
    wide[...] = pre.astype(jnp.bfloat16).astype(jnp.float32)
    acc = bias_ref[...]
    for k in range(taps):
        acc = acc + taps_ref[k : k + 1, :] * wide[pl.ds(HALO - taps + 1 + k, span), :conv_width]
    conv = (acc * jax.nn.sigmoid(acc)).astype(jnp.bfloat16)
    b = conv[:, :state]
    c = conv[:, state : 2 * state]
    x = conv[:, 2 * state :]
    c_ref[...] = c
    raw = wide[HALO:, conv_width:]
    dt = jax.nn.softplus(raw + dtb_ref[...])
    row = lax.broadcasted_iota(jnp.int32, (span, span), 0)
    col = lax.broadcasted_iota(jnp.int32, (span, span), 1)
    causal = row >= col
    cum = jnp.dot(
        causal.astype(jnp.float32),
        dt * rate_ref[...],
        preferred_element_type=jnp.float32,
        precision=lax.Precision.HIGHEST,
    )
    cum_ref[...] = cum
    cum_t = cum.T
    dt_t = dt.T
    inner_dots = lax.dot_general(
        c, b, (((1,), (1,)), ((), ())), preferred_element_type=jnp.float32
    )
    inner_dots = jnp.where(causal, inner_dots, 0.0)
    parts = []
    for h in range(heads):
        gap = cum_t[h : h + 1, :] - cum[:, h : h + 1]
        scores = inner_dots * jnp.exp(jnp.minimum(gap, 0.0)) * dt_t[h : h + 1, :]
        parts.append(
            jnp.dot(
                scores.astype(jnp.bfloat16),
                x[:, h * HEADDIM : (h + 1) * HEADDIM],
                preferred_element_type=jnp.float32,
            )
        )
    x32 = x.astype(jnp.float32)
    y_ref[...] = jnp.concatenate(parts, axis=1) + skip_ref[...] * x32
    to_end = jnp.exp(cum - cum[span - 1 : span, :]) * dt
    weighted = (x32 * spread(to_end, heads)).astype(jnp.bfloat16)
    st_ref[...] = lax.dot_general(
        b, weighted, (((0,), (0,)), ((), ())), preferred_element_type=jnp.float32
    )


def pair_kernel(heads, place_ref, *refs):
    out_ref = refs[-1]
    a_first = place_ref[0] == 0
    for m in range(out_ref.shape[0]):
        st_a, st_b, cum_a, cum_b = refs[4 * m : 4 * m + 4]
        span = cum_a.shape[0]
        state = st_a.shape[0]
        end_a = jnp.exp(-spread(cum_a[span - 1 : span, :], heads))
        end_b = jnp.exp(-spread(cum_b[span - 1 : span, :], heads))
        scale_a = jnp.where(a_first, end_b, 1.0)
        scale_b = jnp.where(a_first, 1.0, end_a)
        pair = st_a[...] * scale_a + st_b[...] * scale_b
        out_ref[m, :state, :] = pair.astype(jnp.bfloat16)
        decay = end_a * end_b
        high = decay.astype(jnp.bfloat16)
        left = decay - high.astype(jnp.float32)
        middle = left.astype(jnp.bfloat16)
        low = (left - middle.astype(jnp.float32)).astype(jnp.bfloat16)
        tail = jnp.broadcast_to(low.astype(jnp.float32), (HALO, decay.shape[1]))
        row = lax.broadcasted_iota(jnp.int32, tail.shape, 0)
        tail = jnp.where(row == 0, high.astype(jnp.float32), tail)
        tail = jnp.where(row == 1, middle.astype(jnp.float32), tail)
        out_ref[m, state:, :] = tail.astype(jnp.bfloat16)


def scan_kernel(depth, groups, place_ref, *refs):
    enter_ref, held = refs[-2:]
    q = place_ref[1]
    z = place_ref[2]
    sections, state, inner = enter_ref.shape
    start = 0
    base = 0
    for size in groups:
        own = refs[base]
        up = refs[base + 1 : base + depth]
        down = refs[base + depth : base + 2 * depth - 1]
        base += 2 * depth - 1
        held[z, start : start + size] = own[...]
        for r in range(1, depth):

            @pl.when(z >= r)
            def _(r=r, up=up, start=start, size=size):
                held[z - r, start : start + size] = up[r - 1][...]

            @pl.when(z + r < depth)
            def _(r=r, down=down, start=start, size=size):
                held[z + r, start : start + size] = down[r - 1][...]

        start += size

    def step(k, running):
        s = k // depth
        zz = k % depth
        mask = s ^ q
        m = place_ref[3 + mask]

        @pl.when(zz == z)
        def _():
            enter_ref[m] = running

        tail = held[zz, m, state:, :].astype(jnp.float32)
        decay = tail[0:1, :] + tail[1:2, :] + tail[2:3, :]
        return running * decay + held[zz, m, :state, :].astype(jnp.float32)

    lax.fori_loop(0, sections * depth, step, jnp.zeros((state, inner), jnp.float32))


def gate_kernel(heads, m, place_ref, rows_a, rows_b, mat_ref, y_a, y_b, c_a, c_b, cum_a, cum_b,
                st_a, st_b, enter_ref, out_ref):
    span = y_a.shape[0]
    a_first = place_ref[0] == 0
    enter = enter_ref[m]
    end_a = jnp.exp(-spread(cum_a[span - 1 : span, :], heads))
    end_b = jnp.exp(-spread(cum_b[span - 1 : span, :], heads))
    in_a = jnp.where(a_first, enter, enter * end_b + st_b[...])
    in_b = jnp.where(a_first, enter * end_a + st_a[...], enter)
    for k, (rows, y, c, cum, start) in enumerate(
        ((rows_a, y_a, c_a, cum_a, in_a), (rows_b, y_b, c_b, cum_b, in_b))
    ):
        z = jnp.dot(rows[HALO:, :], mat_ref[...], preferred_element_type=jnp.float32)
        gate = z.astype(jnp.bfloat16).astype(jnp.float32)
        reached = jnp.dot(
            c[...], start.astype(jnp.bfloat16), preferred_element_type=jnp.float32
        )
        total = y[...] + reached * spread(jnp.exp(-cum[...]), heads)
        out_ref[k] = (total * gate * jax.nn.sigmoid(gate)).astype(jnp.bfloat16)


def norm_kernel(masks, place_ref, *refs):
    gain_ref, out_ref = refs[-2:]
    pieces = refs[:-2]
    c = place_ref[0]
    q = place_ref[1]
    part = pieces[0].shape[-1]
    values = [r[...].astype(jnp.float32) for r in pieces]
    total = sum(jnp.sum(v * v, axis=-1, keepdims=True) for v in values)
    scale = lax.rsqrt(total / (part * len(pieces)) + EPS)
    values = [v * scale for v in values]
    cores = len(masks)
    for here in range(cores):
        for s in range(len(pieces) // cores):

            @pl.when((q == s) & (c == here))
            def _(here=here, s=s):
                for m in range(len(masks[0])):
                    for k in range(cores):
                        core = here ^ k
                        group = (s ^ masks[core][m]) * cores + core
                        first = group * part
                        out_ref[:, first : first + part] = (
                            values[m * cores + k] * gain_ref[:, first : first + part]
                        ).astype(jnp.bfloat16)


def per_device(
    tokens,
    pre_gain,
    w_z,
    w_x,
    w_bc,
    w_dt,
    conv_weight,
    conv_bias,
    dt_bias,
    a_log,
    d_skip,
    norm_gain,
):
    sections, depth, cores = (lax.axis_size(axis) for axis in ALL)
    q, z, c = (lax.axis_index(axis) for axis in ALL)
    span, width = tokens.shape
    state = w_bc.shape[1] // 2
    heads = a_log.shape[0] // (sections * cores)
    inner = heads * HEADDIM
    group = q * cores + c
    smem = pl.BlockSpec(memory_space=pltpu.SMEM)
    vmem = pl.BlockSpec(memory_space=pltpu.VMEM)
    masks = ((0, 2, 1, 3), (0, 1, 2, 3))
    order = [jnp.where(c == 0, masks[0].index(k), masks[1].index(k)) for k in range(sections)]
    place = jnp.stack([c, q, z] + order).astype(jnp.int32)

    small = jnp.concatenate([w_bc, w_dt], 1)
    share = small.shape[0] // sections
    small = lax.dynamic_slice_in_dim(small, q * share, share, 0)
    small = [small] + [
        lax.ppermute(small, "zed", [(i, (i + r) % depth) for i in range(depth)])
        for r in range(1, depth)
    ]
    small = jnp.stack(small)
    small = [small] + [routed(small, (masks[0][m], masks[1][m])) for m in range(1, sections)]
    small = jnp.stack(small)
    small = [small, swapped(small, "core", 1)]

    before = following(tokens[span - HALO :])
    normed = rms_scale(tokens.astype(jnp.float32), pre_gain).astype(jnp.bfloat16)
    halo = rms_scale(before.astype(jnp.float32), pre_gain).astype(jnp.bfloat16)
    own = jnp.concatenate([halo, normed], 0)
    first_hop = routed(own, (masks[0][1], masks[1][1]))
    second_hop = routed(own, (masks[0][2], masks[1][2]))
    diagonal = routed(first_hop, (masks[0][2], masks[1][2]))
    rows_mine = [own, first_hop, second_hop, diagonal]
    crossed = [swapped(v, "core", 1) for v in rows_mine]
    rows_other = [crossed[0], crossed[2], crossed[1], crossed[3]]

    def columns(matrix):
        mine = lax.dynamic_slice_in_dim(matrix, q * (cores * inner), cores * inner, 1)
        keep = jnp.where(c == 0, mine[:, :inner], mine[:, inner:])
        give = jnp.where(c == 0, mine[:, inner:], mine[:, :inner])
        got = swapped(give, "core", 1)
        low = jnp.where(c == 0, keep, got)
        high = jnp.where(c == 0, got, keep)
        up, down = line_gather(jnp.concatenate([low, high], 0), "zed")
        return placed_line(up, down, "zed").reshape(width, inner)

    full_x = columns(w_x)
    full_z = columns(w_z)

    full_small = jnp.zeros((depth, cores, sections, share, small[0].shape[-1]), w_bc.dtype)
    for k in range(cores):
        core = c ^ k
        for m in range(sections):
            section = q ^ jnp.where(core == 0, masks[0][m], masks[1][m])
            for r in range(depth):
                full_small = lax.dynamic_update_slice(
                    full_small,
                    small[k][m, r][None, None, None],
                    ((z - r) % depth, core, section, 0, 0),
                )
    full_small = full_small.reshape(width, -1)
    first = group * heads
    full_dt = lax.dynamic_slice_in_dim(full_small, 2 * state + first, heads, 1)
    full_pre = jnp.concatenate([full_small[:, : 2 * state], full_x, full_dt], 1)

    def mine(vector):
        return lax.dynamic_slice_in_dim(vector, first, heads, 0)[None, :]

    def channels(matrix):
        x_side = lax.dynamic_slice_in_dim(matrix, group * inner, inner, 1)
        return jnp.concatenate([matrix[:, -2 * state :], x_side], 1)

    taps = channels(conv_weight)
    bias = channels(conv_bias[None, :])
    dtb = mine(dt_bias)
    rate = jnp.exp(mine(a_log))
    skip = jnp.repeat(mine(d_skip), HEADDIM, axis=1)

    def block(rows):
        return pl.pallas_call(
            functools.partial(block_kernel, heads, state),
            out_shape=(
                jax.ShapeDtypeStruct((span, inner), jnp.float32),
                jax.ShapeDtypeStruct((span, state), jnp.bfloat16),
                jax.ShapeDtypeStruct((span, heads), jnp.float32),
                jax.ShapeDtypeStruct((state, inner), jnp.float32),
            ),
            scratch_shapes=[pltpu.VMEM((span + HALO, full_pre.shape[1]), jnp.float32)],
            compiler_params=params(),
        )(rows, full_pre, taps, bias, dtb, rate, skip)

    terms_mine = [block(rows) for rows in rows_mine]
    terms_other = [block(rows) for rows in rows_other]

    groups = (sections - 1, 1)
    gathered = []
    start = 0
    for size in groups:
        operands = []
        for m in range(start, start + size):
            (_, _, cum_a, st_a), (_, _, cum_b, st_b) = terms_mine[m], terms_other[m]
            operands += [st_a, st_b, cum_a, cum_b]
        start += size
        pair = pl.pallas_call(
            functools.partial(pair_kernel, heads),
            out_shape=jax.ShapeDtypeStruct((size, state + HALO, inner), jnp.bfloat16),
            in_specs=[smem] + [vmem] * len(operands),
            compiler_params=params(),
        )(place, *operands)
        up, down = line_gather(pair, "zed")
        gathered += up + down[1:]
    enter = pl.pallas_call(
        functools.partial(scan_kernel, depth, groups),
        out_shape=jax.ShapeDtypeStruct((sections, state, inner), jnp.float32),
        in_specs=[smem] + [vmem] * len(gathered),
        scratch_shapes=[pltpu.VMEM((depth, sections, state + HALO, inner), jnp.bfloat16)],
        compiler_params=params(),
    )(place, *gathered)

    pieces = [None] * (sections * cores)
    for m in (3, 1, 2, 0):
        (y_a, c_a, cum_a, st_a), (y_b, c_b, cum_b, st_b) = terms_mine[m], terms_other[m]
        gated = pl.pallas_call(
            functools.partial(gate_kernel, heads, m),
            out_shape=jax.ShapeDtypeStruct((cores, span, inner), jnp.bfloat16),
            in_specs=[smem] + [vmem] * 12,
            compiler_params=params(),
        )(place, rows_mine[m], rows_other[m], full_z, y_a, y_b, c_a, c_b, cum_a, cum_b,
          st_a, st_b, enter)
        if m:
            gated = routed(gated, (masks[0][m], masks[1][m]))
        pieces[m * cores] = gated[0]
        pieces[m * cores + 1] = swapped(gated[1], "core", 1)
    return pl.pallas_call(
        functools.partial(norm_kernel, masks),
        out_shape=jax.ShapeDtypeStruct((span, sections * cores * inner), jnp.bfloat16),
        in_specs=[smem] + [vmem] * (len(pieces) + 1),
        compiler_params=params(),
    )(place, *pieces, norm_gain[None, :])


def solution(mesh):
    sections, fsdp = (mesh.shape[axis] for axis in ("sec", "fsdp"))
    split = Mesh(mesh.devices.reshape(sections, fsdp // 2, 2), ALL)
    rows = P(("zed", "core"), None)
    placed = (P(ALL, None), P(), rows, rows, rows, rows, P(), P(), P(), P(), P(), P())
    return jax.shard_map(
        per_device, mesh=split, in_specs=placed, out_specs=P(ALL, None), check_vma=False
    )
```

```python
import functools
import jax
import jax.numpy as jnp
from jax import lax
from jax.experimental import pallas as pl
from jax.experimental.pallas import tpu as pltpu
from jax.sharding import Mesh, PartitionSpec as P

HEADDIM = 64
EPS = 1e-05
HALO = 16
LANES = 128
VMEM_LIMIT = 32 * 1024 * 1024
ALL = ("sec", "zed", "core")


def params():
    return pltpu.CompilerParams(vmem_limit_bytes=VMEM_LIMIT)


def swapped(value, axis, mask):
    count = lax.axis_size(axis)
    return lax.ppermute(value, axis, [(i, i ^ mask) for i in range(count)])


def routed(value, masks):
    sections, depth, cores = (lax.axis_size(axis) for axis in ALL)
    pairs = []
    for s in range(sections):
        for z in range(depth):
            for c in range(cores):
                place = z * cores + c
                pairs.append(
                    (s * depth * cores + place, (s ^ masks[c]) * depth * cores + place)
                )
    return lax.ppermute(value, ALL, pairs)


def before_chip(tail):
    sections, depth, cores = (lax.axis_size(axis) for axis in ALL)
    chips = sections * depth
    return lax.ppermute(
        tail, ALL, [(i * cores + cores - 1, (i + 1) * cores) for i in range(chips - 1)]
    )


def around(value, axis):
    count = lax.axis_size(axis)
    return [value] + [
        lax.ppermute(value, axis, [(i, (i + r) % count) for i in range(count)])
        for r in range(1, count)
    ]


def spread(columns, heads):
    rows = columns.shape[0]
    return jnp.concatenate(
        [jnp.broadcast_to(columns[:, h : h + 1], (rows, HEADDIM)) for h in range(heads)],
        axis=1,
    )


def window(c, inner):
    shift = inner % LANES
    width = -(-(inner + shift) // LANES) * LANES
    return pl.multiple_of(c * (inner - shift), LANES), width, shift


def chosen(wide, c, inner, shift):
    return jnp.where(c == 0, wide[:, :inner], wide[:, shift : shift + inner])


def share_of(height, sections):
    return -(-height // (sections * HALO)) * HALO


def share_start(section, height, share):
    return jnp.minimum(section * share, height - share)


def matrix_kernel(masks, inner, state, height, place_ref, mine_ref, other_ref, both_ref, out_ref,
                  arrived):
    c = place_ref[0]
    q = place_ref[1]
    z = place_ref[2]
    first, width, _ = window(c, inner)
    copy = pltpu.make_async_copy(
        both_ref.at[:, pl.ds(first, width)], out_ref.at[:, :width], arrived
    )
    copy.start()
    sections, _, lanes = mine_ref.shape
    cores = 2
    depth = out_ref.shape[0] // (cores * height)
    share = share_of(height, sections)
    steps = lanes - 2 * state
    for k, ref in enumerate((mine_ref, other_ref)):
        core = c ^ k
        for m in range(sections):
            section = q ^ jnp.where(core == 0, masks[0][m], masks[1][m])
            for r in range(depth):
                block = ((z + depth - r) % depth) * cores + core
                first_row = block * height + share_start(section, height, share)
                rows = pl.ds(pl.multiple_of(first_row, HALO), share)
                here = slice(r * share, (r + 1) * share)
                out_ref[rows, width : width + steps] = ref[m, here, 2 * state :]
                out_ref[rows, width + steps :] = ref[m, here, : 2 * state]
    copy.wait()


def conv_silu(wide, taps_ref, bias_ref, span):
    taps = taps_ref.shape[0]
    acc = bias_ref[...]
    for k in range(taps):
        acc = acc + taps_ref[k : k + 1, :] * wide[pl.ds(HALO - taps + 1 + k, span), :]
    return (acc * jax.nn.sigmoid(acc)).astype(jnp.bfloat16)


def block_terms(heads, b, c_conv, x, dt, cum, lower, skip):
    span = b.shape[0]
    cum_t = cum.T
    dt_t = dt.T
    inner_dots = lax.dot_general(
        c_conv, b, (((1,), (1,)), ((), ())), preferred_element_type=jnp.float32
    )
    inner_dots = inner_dots * lower
    half = span // 2
    parts = []
    for h in range(heads):
        x_head = x[:, h * HEADDIM : (h + 1) * HEADDIM]
        rows_of = []
        for low_row, high_row in ((0, half), (half, span)):
            gap = cum_t[h : h + 1, :high_row] - cum[low_row:high_row, h : h + 1]
            scores = (
                inner_dots[low_row:high_row, :high_row]
                * jnp.exp(jnp.minimum(gap, 0.0))
                * dt_t[h : h + 1, :high_row]
            )
            rows_of.append(
                jnp.dot(
                    scores.astype(jnp.bfloat16),
                    x_head[:high_row],
                    preferred_element_type=jnp.float32,
                )
            )
        parts.append(jnp.concatenate(rows_of, 0))
    x32 = x.astype(jnp.float32)
    y = jnp.concatenate(parts, axis=1) + skip * x32
    to_end = jnp.exp(cum - cum[span - 1 : span, :]) * dt
    weighted = (x32 * spread(to_end, heads)).astype(jnp.bfloat16)
    st = lax.dot_general(
        b, weighted, (((0,), (0,)), ((), ())), preferred_element_type=jnp.float32
    )
    return y, st


def chunk_kernel(heads, state, chunks, place_ref, *refs):
    count = len(chunks)
    rows_mine, rows_other = refs[:count], refs[count : 2 * count]
    (halo_mine, halo_other, mat_ref, pick_ref, taps_ref, bias_ref, dtb_ref, rate_ref, skip_ref,
     y_ref, c_ref, cum_ref, st_ref, pair_ref, held, halo, wide, lower_ref, scale_ref, dt_ref,
     conv_ref, arrived) = refs[2 * count :]
    c = place_ref[0]
    cores, span = y_ref.shape[1:3]
    inner = heads * HEADDIM
    model = held.shape[2]
    lanes = halo.shape[2]
    pieces = -(-model // lanes)
    extra = halo_mine.shape[1] - pieces * HALO

    def rows_copies(i, slot):
        copies = []
        for k, rows in enumerate((rows_mine[i], rows_other[i])):
            first = pl.multiple_of(HALO + (c ^ k) * span, HALO)
            copies.append(
                pltpu.make_async_copy(
                    rows, held.at[slot, pl.ds(first, span)], arrived.at[slot, 1 + k]
                )
            )
        return copies

    def halo_copy(i, slot, core):
        source, m = ((halo_mine, chunks[i][0]), (halo_other, chunks[i][1]))[core]
        return pltpu.make_async_copy(
            source.at[m, pl.ds(extra, pieces * HALO)], halo.at[slot], arrived.at[slot, 0]
        )

    def start(i):
        for copy in rows_copies(i, i % 2):
            copy.start()
        for core in range(cores):

            @pl.when(c == core)
            def _(core=core):
                halo_copy(i, i % 2, core).start()

    start(0)
    row = lax.broadcasted_iota(jnp.int32, (span, span), 0)
    col = lax.broadcasted_iota(jnp.int32, (span, span), 1)
    lower_ref[...] = (row >= col).astype(jnp.float32)
    _, width, shift = window(c, inner)
    steps = mat_ref.shape[1] - width - 2 * state

    def one_chunk(i, carry):
        for j in range(1, count):

            @pl.when(i + 1 == j)
            def _(j=j):
                start(j)

        slot = i % 2
        for copy in rows_copies(0, slot):
            copy.wait()
        halo_copy(0, slot, 0).wait()
        for j in range(pieces):
            last = min(lanes, model - j * lanes)
            held[slot, :HALO, j * lanes : j * lanes + last] = halo[
                slot, j * HALO : (j + 1) * HALO, :last
            ]
        rows = held[slot]
        values = rows.astype(jnp.float32)
        scale = lax.rsqrt(jnp.mean(values * values, axis=-1, keepdims=True) + EPS)
        total = jnp.dot(rows, mat_ref[...], preferred_element_type=jnp.float32)
        pre = (total * scale).astype(jnp.bfloat16)
        wide[:, : 2 * state] = pre[:, width + steps :].astype(jnp.float32)
        wide[:, 2 * state :] = chosen(pre.astype(jnp.float32), c, inner, shift)
        raw = jnp.dot(
            pre[HALO:, width : width + steps], pick_ref[...], preferred_element_type=jnp.float32
        )
        scale_ref[...] = scale[HALO:]
        dt_ref[...] = jax.nn.softplus(raw + dtb_ref[...])
        conv_ref[...] = conv_silu(wide, taps_ref, bias_ref, cores * span)

        def one_block(k, before):
            here = pl.ds(pl.multiple_of(k * span, span), span)
            dt = dt_ref[here, :]
            rise = dt * rate_ref[...]
            high = rise.astype(jnp.bfloat16)
            left = rise - high.astype(jnp.float32)
            middle = left.astype(jnp.bfloat16)
            low = (left - middle.astype(jnp.float32)).astype(jnp.bfloat16)
            lower = lower_ref[...]
            cum = sum(
                jnp.dot(lower.astype(jnp.bfloat16), part, preferred_element_type=jnp.float32)
                for part in (low, middle, high)
            )
            b = conv_ref[here, :state]
            c_conv = conv_ref[here, state : 2 * state]
            x = conv_ref[here, 2 * state :]
            y, st = block_terms(heads, b, c_conv, x, dt, cum, lower, skip_ref[...])
            y_ref[i, k] = y
            c_ref[i, k] = c_conv
            cum_ref[i, k, :, :heads] = cum
            cum_ref[i, k, :, heads:] = scale_ref[here, :]
            st_ref[i, k] = st
            end = jnp.exp(-spread(cum[span - 1 : span, :], heads))
            return before[0] * end + st, before[1] * end

        joined, decay = lax.fori_loop(
            0,
            cores,
            one_block,
            (jnp.zeros((state, inner), jnp.float32), jnp.ones((1, inner), jnp.float32)),
        )
        store_joined(pair_ref, i, joined, decay)
        return carry

    lax.fori_loop(0, count, one_chunk, 0)


def store_joined(out_ref, m, pair, decay):
    state = pair.shape[0]
    out_ref[m, :state, :] = pair.astype(jnp.bfloat16)
    high = decay.astype(jnp.bfloat16)
    left = decay - high.astype(jnp.float32)
    middle = left.astype(jnp.bfloat16)
    low = (left - middle.astype(jnp.float32)).astype(jnp.bfloat16)
    tail = jnp.broadcast_to(low.astype(jnp.float32), (HALO, decay.shape[1]))
    row = lax.broadcasted_iota(jnp.int32, tail.shape, 0)
    tail = jnp.where(row == 0, high.astype(jnp.float32), tail)
    tail = jnp.where(row == 1, middle.astype(jnp.float32), tail)
    out_ref[m, state:, :] = tail.astype(jnp.bfloat16)


def load_joined(ref, *index):
    state = ref.shape[-2] - HALO
    tail = ref[index + (slice(state, None),)].astype(jnp.float32)
    decay = tail[0:1, :] + tail[1:2, :] + tail[2:3, :]
    return ref[index + (slice(0, state),)].astype(jnp.float32), decay


def join_kernel(place_ref, mine_ref, other_ref, out_ref):
    mine_first = place_ref[2] % 2 == 0
    for m in range(out_ref.shape[0]):
        own, own_decay = load_joined(mine_ref, m)
        other, other_decay = load_joined(other_ref, m)
        joined = own * jnp.where(mine_first, other_decay, 1.0) + other * jnp.where(
            mine_first, 1.0, own_decay
        )
        store_joined(out_ref, m, joined, own_decay * other_decay)


def scan_kernel(depth, groups, place_ref, *refs):
    enter_ref, held, beside = refs[-3:]
    q = place_ref[1]
    z = place_ref[2]
    sections, state, inner = enter_ref.shape
    pairs = depth // 2
    start = 0
    base = 0
    for size in groups:
        part = slice(start, start + size)
        beside[part] = refs[base][...]
        held[z // 2, part] = refs[base + 1][...]
        for r in range(1, depth - 1):
            ref = refs[base + 1 + r]
            rising = (z - r) % 2 == 1

            @pl.when(rising & (z > r))
            def _(ref=ref, part=part, r=r):
                held[(z - r - 1) // 2, part] = ref[...]

            @pl.when(jnp.logical_not(rising) & (z + r < depth - 1))
            def _(ref=ref, part=part, r=r):
                held[(z + r) // 2, part] = ref[...]

        base += depth
        start += size

    def step(k, running):
        s = k // pairs
        pair = k % pairs
        mask = s ^ q
        m = place_ref[3 + mask]

        @pl.when((pair == z // 2) & (z % 2 == 0))
        def _():
            enter_ref[m] = running

        @pl.when((pair == z // 2) & (z % 2 == 1))
        def _():
            first, decay = load_joined(beside, m)
            enter_ref[m] = running * decay + first

        joined, decay = load_joined(held, pair, m)
        return running * decay + joined

    lax.fori_loop(0, sections * pairs, step, jnp.zeros((state, inner), jnp.float32))


def silu_kernel(heads, place_ref, *refs):
    both_ref, out_ref, held, arrived = refs[-4:]
    count = out_ref.shape[0]
    rows, groups = refs[:count], refs[count:-4]
    cums = [(ref, i) for ref in groups for i in range(ref.shape[0])]
    c = place_ref[0]
    inner = heads * HEADDIM
    first, width, shift = window(c, inner)

    def copy(k):
        return pltpu.make_async_copy(rows[k], held.at[k % 2], arrived.at[k % 2])

    copy(0).start()
    for k in range(count):
        if k + 1 < count:
            copy(k + 1).start()
        copy(k).wait()
        wide = jnp.dot(
            held[k % 2], both_ref[:, pl.ds(first, width)], preferred_element_type=jnp.float32
        )
        block = c ^ (k % 2)
        ref, i = cums[k // 2]
        scale = ref[i, block][:, heads:]
        gate = (chosen(wide, c, inner, shift) * scale).astype(jnp.bfloat16).astype(jnp.float32)
        out_ref[k // 2 * 2 + block] = gate * jax.nn.sigmoid(gate)


def gate_kernel(heads, m, i, place_ref, silu_ref, y_ref, c_ref, cum_ref, st_ref, enter_ref,
                out_ref):
    span = y_ref.shape[2]
    c = place_ref[0]
    enter = enter_ref[m]
    end = jnp.exp(-spread(cum_ref[i, 0, span - 1 : span, :heads], heads))
    starts = (enter, enter * end + st_ref[i, 0])
    for k, start in enumerate(starts):
        reached = jnp.dot(
            c_ref[i, k], start.astype(jnp.bfloat16), preferred_element_type=jnp.float32
        )
        total = y_ref[i, k] + reached * spread(jnp.exp(-cum_ref[i, k, :, :heads]), heads)
        out_ref[c ^ k] = (total * silu_ref[2 * m + k]).astype(jnp.bfloat16)


def norm_kernel(masks, place_ref, *refs):
    gain_ref, out_ref = refs[-2:]
    pieces = refs[:-2]
    c = place_ref[0]
    q = place_ref[1]
    part = pieces[0].shape[-1]
    values = [r[...].astype(jnp.float32) for r in pieces]
    total = sum(jnp.sum(v * v, axis=-1, keepdims=True) for v in values)
    scale = lax.rsqrt(total / (part * len(pieces)) + EPS)
    values = [v * scale for v in values]
    cores = len(masks)
    for here in range(cores):
        for s in range(len(pieces) // cores):

            @pl.when((q == s) & (c == here))
            def _(here=here, s=s):
                for m in range(len(masks[0])):
                    for k in range(cores):
                        core = here ^ k
                        group = (s ^ masks[core][m]) * cores + core
                        first = group * part
                        out_ref[:, first : first + part] = (
                            values[m * cores + k] * gain_ref[:, first : first + part]
                        ).astype(jnp.bfloat16)


def per_device(
    tokens,
    pre_gain,
    w_z,
    w_x,
    w_bc,
    w_dt,
    conv_weight,
    conv_bias,
    dt_bias,
    a_log,
    d_skip,
    norm_gain,
):
    sections, depth, cores = (lax.axis_size(axis) for axis in ALL)
    q, z, c = (lax.axis_index(axis) for axis in ALL)
    span, width = tokens.shape
    state = w_bc.shape[1] // 2
    heads = a_log.shape[0] // (sections * cores)
    inner = heads * HEADDIM
    group = q * cores + c
    smem = pl.BlockSpec(memory_space=pltpu.SMEM)
    vmem = pl.BlockSpec(memory_space=pltpu.VMEM)
    masks = ((0, 2, 1, 3), (0, 1, 2, 3))
    order = [jnp.where(c == 0, masks[0].index(k), masks[1].index(k)) for k in range(sections)]
    place = jnp.stack([c, q, z] + order).astype(jnp.int32)

    hbm = pl.BlockSpec(memory_space=pltpu.HBM)

    def call(kernel, out_shape, *operands, scratch=(), scalars=False, far=()):
        return pl.pallas_call(
            kernel,
            out_shape=out_shape,
            in_specs=[
                smem if scalars and i == 0 else hbm if i in far else vmem
                for i in range(len(operands))
            ],
            scratch_shapes=list(scratch),
            compiler_params=params(),
        )(*operands)

    height = w_x.shape[0]
    mine_gain = lax.dynamic_slice_in_dim(pre_gain, (z * cores + c) * height, height, 0)

    def scaled(matrix, gain):
        return (matrix.astype(jnp.float32) * gain[:, None]).astype(jnp.bfloat16)

    def quarter(matrix):
        own = lax.dynamic_slice_in_dim(matrix, q * (cores * inner), cores * inner, 1)
        return scaled(own, mine_gain)

    both_x = lax.all_gather(quarter(w_x), ("zed", "core"), axis=0, tiled=True)
    both_z = lax.all_gather(quarter(w_z), ("zed", "core"), axis=0, tiled=True)

    share = share_of(height, sections)
    start = share_start(q, height, share)
    small = jnp.concatenate([w_bc, w_dt], 1)
    small = lax.dynamic_slice_in_dim(small, start, share, 0)
    small = scaled(small, lax.dynamic_slice_in_dim(mine_gain, start, share, 0))
    lanes = -(-small.shape[1] // LANES) * LANES
    small = jnp.pad(small, ((0, 0), (0, lanes - small.shape[1])))
    halo = jnp.pad(before_chip(tokens[span - HALO :]), ((0, 0), (0, -width % lanes)))
    halo = [halo[:, i : i + lanes] for i in range(0, halo.shape[1], lanes)]
    bundle = jnp.concatenate(around(small, "zed") + halo, 0)

    first_hop = routed(tokens, (masks[0][1], masks[1][1]))
    later, bundle = lax.optimization_barrier((tokens, bundle))
    bundle = jnp.stack(
        [bundle] + [routed(bundle, (masks[0][m], masks[1][m])) for m in range(1, sections)]
    )
    second_hop = routed(later, (masks[0][2], masks[1][2]))
    diagonal = routed(first_hop, (masks[0][2], masks[1][2]))
    rows_mine = [tokens, first_hop, second_hop, diagonal]
    bundles = [bundle, swapped(bundle, "core", 1)]

    first = group * heads
    (dt_bias, a_log, d_skip, conv_weight, conv_bias), _ = lax.optimization_barrier(
        ((dt_bias, a_log, d_skip, conv_weight, conv_bias), bundle)
    )

    def mine(vector):
        return lax.dynamic_slice_in_dim(vector, first, heads, 0)[None, :]

    def channels(matrix):
        x_side = lax.dynamic_slice_in_dim(matrix, group * inner, inner, 1)
        return jnp.concatenate([matrix[:, -2 * state :], x_side], 1)

    dtb = mine(dt_bias)
    rate = jnp.exp(mine(a_log))
    skip = jnp.repeat(mine(d_skip), HEADDIM, axis=1)
    taps, bias = channels(conv_weight), channels(conv_bias[None, :])
    steps = lanes - 2 * state
    pick = (
        lax.broadcasted_iota(jnp.int32, (steps, heads), 0)
        == lax.broadcasted_iota(jnp.int32, (steps, heads), 1) + first
    ).astype(jnp.bfloat16)
    matrix = call(
        functools.partial(matrix_kernel, masks, inner, state, height),
        jax.ShapeDtypeStruct((width, window(0, inner)[1] + lanes), jnp.bfloat16),
        place,
        *bundles,
        both_x,
        scratch=[pltpu.SemaphoreType.DMA],
        scalars=True,
        far=(3,),
    )

    def group_terms(chunks, mine, other):
        n = len(chunks)
        return call(
            functools.partial(
                chunk_kernel, heads, state, [(m, masks[0].index(masks[1][m])) for m in chunks]
            ),
            (
                jax.ShapeDtypeStruct((n, cores, span, inner), jnp.float32),
                jax.ShapeDtypeStruct((n, cores, span, state), jnp.bfloat16),
                jax.ShapeDtypeStruct((n, cores, span, heads + 1), jnp.float32),
                jax.ShapeDtypeStruct((n, cores, state, inner), jnp.float32),
                jax.ShapeDtypeStruct((n, state + HALO, inner), jnp.bfloat16),
            ),
            place, *mine, *other, *bundles, matrix, pick, taps, bias, dtb, rate, skip,
            scratch=[
                pltpu.VMEM((2, HALO + cores * span, width), jnp.bfloat16),
                pltpu.VMEM((2, -(-width // lanes) * HALO, lanes), jnp.bfloat16),
                pltpu.VMEM((HALO + cores * span, 2 * state + inner), jnp.float32),
                pltpu.VMEM((span, span), jnp.float32),
                pltpu.VMEM((cores * span, 1), jnp.float32),
                pltpu.VMEM((cores * span, heads), jnp.float32),
                pltpu.VMEM((cores * span, 2 * state + inner), jnp.bfloat16),
                pltpu.SemaphoreType.DMA((2, 1 + cores)),
            ],
            scalars=True,
            far=range(1, 1 + 2 * n + 2),
        )

    groups = (sections - 1, 1)
    crossed = [swapped(v, "core", 1) for v in rows_mine[:-1]]
    rows_other = [crossed[0], crossed[2], crossed[1]]
    terms = [group_terms((0, 1, 2), rows_mine[:-1], rows_other)]
    diagonal, _ = lax.optimization_barrier((diagonal, terms[0][-1]))
    rows_mine[-1] = diagonal
    rows_other.append(swapped(diagonal, "core", 1))
    terms.append(group_terms((3,), rows_mine[-1:], rows_other[-1:]))

    def neighbours(r):
        pairs = []
        for i in range(depth):
            rising = (i - r + 1) % 2 == 1
            if rising and i - r + 1 >= 1 and i + 1 < depth:
                pairs.append((i, i + 1))
            if not rising and i + r - 1 <= depth - 2 and i >= 1:
                pairs.append((i, i - 1))
        return pairs

    gathered = []
    for size, (*_, own_pair) in zip(groups, terms):
        shape = jax.ShapeDtypeStruct((size, state + HALO, inner), jnp.bfloat16)
        beside = swapped(own_pair, "zed", 1)
        beside, _ = lax.optimization_barrier((beside, terms[-1][-1]))
        message = call(join_kernel, shape, place, own_pair, beside, scalars=True)
        gathered += [beside, message]
        for r in range(1, depth - 1):
            message = lax.ppermute(message, "zed", neighbours(r))
            gathered.append(message)
    enter = call(
        functools.partial(scan_kernel, depth, groups),
        jax.ShapeDtypeStruct((sections, state, inner), jnp.float32),
        place,
        *gathered,
        scratch=[
            pltpu.VMEM((depth // 2, sections, state + HALO, inner), jnp.bfloat16),
            pltpu.VMEM((sections, state + HALO, inner), jnp.bfloat16),
        ],
        scalars=True,
    )

    every_row = [rows for pair in zip(rows_mine, rows_other) for rows in pair]
    silu = call(
        functools.partial(silu_kernel, heads),
        jax.ShapeDtypeStruct((len(every_row), span, inner), jnp.float32),
        place,
        *every_row,
        *[t[2] for t in terms],
        both_z,
        scratch=[
            pltpu.VMEM((2, span, width), jnp.bfloat16),
            pltpu.SemaphoreType.DMA((2,)),
        ],
        scalars=True,
        far=range(1, 1 + len(every_row)),
    )
    pieces = [None] * (sections * cores)
    for m in (3, 1, 2, 0):
        part, i = (0, m) if m < groups[0] else (1, m - groups[0])
        y, c_conv, cum, st, _ = terms[part]
        gated = call(
            functools.partial(gate_kernel, heads, m, i),
            jax.ShapeDtypeStruct((cores, span, inner), jnp.bfloat16),
            place, silu, y, c_conv, cum, st, enter,
            scalars=True,
        )
        if m:
            gated = routed(gated, (masks[0][m], masks[1][m]))
        pieces[m * cores] = gated[0]
        pieces[m * cores + 1] = swapped(gated[1], "core", 1)
    return call(
        functools.partial(norm_kernel, masks),
        jax.ShapeDtypeStruct((span, sections * cores * inner), jnp.bfloat16),
        place,
        *pieces,
        norm_gain[None, :],
        scalars=True,
    )


def solution(mesh):
    sections, fsdp = (mesh.shape[axis] for axis in ("sec", "fsdp"))
    split = Mesh(mesh.devices.reshape(sections, fsdp // 2, 2), ALL)
    rows = P(("zed", "core"), None)
    placed = (P(ALL, None), P(), rows, rows, rows, rows, P(), P(), P(), P(), P(), P())
    return jax.shard_map(
        per_device, mesh=split, in_specs=placed, out_specs=P(ALL, None), check_vma=False
    )
```

```python
import functools
import jax
import jax.numpy as jnp
from jax import lax
from jax.experimental import pallas as pl
from jax.experimental.pallas import tpu as pltpu
from jax.sharding import Mesh, PartitionSpec as P

HEADDIM = 64
EPS = 1e-05
HALO = 16
LANES = 128
VMEM_LIMIT = 22 * 1024 * 1024
ALL = ("sec", "zed", "core")


def params():
    return pltpu.CompilerParams(vmem_limit_bytes=VMEM_LIMIT)


def swapped(value, axis, mask):
    count = lax.axis_size(axis)
    return lax.ppermute(value, axis, [(i, i ^ mask) for i in range(count)])


def routed(value, masks):
    sections, depth, cores = (lax.axis_size(axis) for axis in ALL)
    pairs = []
    for s in range(sections):
        for z in range(depth):
            for c in range(cores):
                if masks[c] is None:
                    continue
                place = z * cores + c
                pairs.append(
                    (s * depth * cores + place, (s ^ masks[c]) * depth * cores + place)
                )
    return lax.ppermute(value, ALL, pairs)


def before_chip(tail):
    sections, depth, cores = (lax.axis_size(axis) for axis in ALL)
    chips = sections * depth
    return lax.ppermute(
        tail, ALL, [(i * cores + cores - 1, (i + 1) * cores) for i in range(chips - 1)]
    )


def split(value):
    high = value.astype(jnp.bfloat16)
    left = value - high.astype(jnp.float32)
    middle = left.astype(jnp.bfloat16)
    low = (left - middle.astype(jnp.float32)).astype(jnp.bfloat16)
    return high, middle, low


def spread(columns, heads):
    rows = columns.shape[0]
    return jnp.concatenate(
        [jnp.broadcast_to(columns[:, h : h + 1], (rows, HEADDIM)) for h in range(heads)],
        axis=1,
    )


def share_of(size, parts):
    return -(-size // (parts * HALO)) * HALO


def share_start(part, size, share):
    return pl.multiple_of(jnp.minimum(part * share, size - share), HALO)


def spread_rows(row, heads):
    return jnp.concatenate(
        [jnp.broadcast_to(row[:, h : h + 1], (HEADDIM, 1)) for h in range(heads)], axis=0
    )


def window(c, inner):
    shift = inner % LANES
    width = -(-(inner + shift) // LANES) * LANES
    return pl.multiple_of(c * (inner - shift), LANES), width, shift


def chosen(wide, c, inner, shift):
    return jnp.where(c == 0, wide[:, :inner], wide[:, shift : shift + inner])


def window_copies(both, columns, held, c, inner, sems):
    lead, rest = columns
    first, width, _ = window(c, inner)
    cuts = [(0, 0, lead), (lead + first, lead, width)]
    cuts.append((both.shape[1] - rest, lead + width, rest))
    copies = []
    for k, (source, target, size) in enumerate(cuts):
        if size:
            copies.append(
                pltpu.make_async_copy(
                    both.at[:, pl.ds(source, size)], held.at[:, pl.ds(target, size)], sems.at[k]
                )
            )
    return copies


def rows_copies(rows_mine, rows_other, held, sems, c, first):
    span = rows_mine.shape[0]
    copies = []
    for k, rows in enumerate((rows_mine, rows_other)):
        start = pl.multiple_of(first + (c ^ k) * span, HALO)
        copies.append(
            pltpu.make_async_copy(rows, held.at[pl.ds(start, span)], sems.at[k])
        )
    return copies


def conv_silu(wide, taps_ref, bias_ref, span):
    taps = taps_ref.shape[0]
    acc = bias_ref[...]
    for k in range(taps):
        acc = acc + taps_ref[k : k + 1, :] * wide[pl.ds(HALO - taps + 1 + k, span), :]
    return (acc * jax.nn.sigmoid(acc)).astype(jnp.bfloat16)


def block_terms(heads, b, c_conv, x, dt, cum, lower, skip):
    span = b.shape[0]
    cum_t = cum.T
    dt_t = dt.T
    inner_dots = lax.dot_general(
        c_conv, b, (((1,), (1,)), ((), ())), preferred_element_type=jnp.float32
    )
    inner_dots = inner_dots * lower
    half = span // 2
    parts = []
    for h in range(heads):
        x_head = x[:, h * HEADDIM : (h + 1) * HEADDIM]
        rows_of = []
        for low_row, high_row in ((0, half), (half, span)):
            gap = cum_t[h : h + 1, :high_row] - cum[low_row:high_row, h : h + 1]
            scores = (
                inner_dots[low_row:high_row, :high_row]
                * jnp.exp(jnp.minimum(gap, 0.0))
                * dt_t[h : h + 1, :high_row]
            )
            rows_of.append(
                jnp.dot(
                    scores.astype(jnp.bfloat16),
                    x_head[:high_row],
                    preferred_element_type=jnp.float32,
                )
            )
        parts.append(jnp.concatenate(rows_of, 0))
    x32 = x.astype(jnp.float32)
    y = jnp.concatenate(parts, axis=1) + skip * x32
    to_end = jnp.exp(cum - cum[span - 1 : span, :]) * dt
    weighted = (x32 * spread(to_end, heads)).astype(jnp.bfloat16)
    st = lax.dot_general(
        weighted, b, (((0,), (0,)), ((), ())), preferred_element_type=jnp.float32
    )
    return y, st


def chunk_kernel(heads, state, chunks, place_ref, *refs):
    count = len(chunks)
    rows_mine, rows_other = refs[:count], refs[count : 2 * count]
    (halo_mine, halo_other, source_ref, pick_ref, taps_ref, bias_ref, dtb_ref, rate_ref, skip_ref,
     y_ref, c_ref, cum_ref, st_ref) = refs[2 * count : 2 * count + 13]
    pair_refs = refs[2 * count + 13 : -11]
    (mat_ref, held, wide, lower_ref, scale_ref, dt_ref, conv_ref, joined_ref, tail_ref, arrived,
     loaded) = refs[-11:]
    c = place_ref[0]
    cores, span = y_ref.shape[1:3]
    inner = heads * HEADDIM
    _, width, shift = window(c, inner)
    steps = mat_ref.shape[1] - width - 2 * state
    depth = len(pair_refs)
    share = share_of(inner, depth)

    def halo_copy(i, slot, core):
        source, m = ((halo_mine, chunks[i][0]), (halo_other, chunks[i][1]))[core]
        return pltpu.make_async_copy(source.at[m], held.at[slot, :HALO], arrived.at[slot, cores])

    def all_rows(i, slot):
        return rows_copies(
            rows_mine[i], rows_other[i], held.at[slot], arrived.at[slot], c, HALO
        )

    def start(i):
        for copy in all_rows(i, i % 2):
            copy.start()
        for core in range(cores):

            @pl.when(c == core)
            def _(core=core):
                halo_copy(i, i % 2, core).start()

    weights = window_copies(source_ref, (2 * state, steps), mat_ref, c, inner, loaded)
    for copy in weights:
        copy.start()
    start(0)
    tail_ref[...] = jnp.zeros_like(tail_ref)
    st_ref[...] = jnp.zeros_like(st_ref)
    row = lax.broadcasted_iota(jnp.int32, (span, span), 0)
    col = lax.broadcasted_iota(jnp.int32, (span, span), 1)
    lower_ref[...] = (row >= col).astype(jnp.float32)
    for copy in weights:
        copy.wait()

    def one_chunk(i, carry):
        for j in range(1, count):

            @pl.when(i + 1 == j)
            def _(j=j):
                start(j)

        slot = i % 2
        for copy in all_rows(0, slot):
            copy.wait()
        halo_copy(0, slot, 0).wait()
        rows = held[slot]
        values = rows.astype(jnp.float32)
        scale = lax.rsqrt(jnp.mean(values * values, axis=-1, keepdims=True) + EPS)
        total = jnp.dot(rows, mat_ref[...], preferred_element_type=jnp.float32)
        pre = (total * scale).astype(jnp.bfloat16)
        wide[:, : 2 * state] = pre[:, : 2 * state].astype(jnp.float32)
        window_part = pre[:, 2 * state : 2 * state + width].astype(jnp.float32)
        wide[:, 2 * state :] = chosen(window_part, c, inner, shift)
        raw = jnp.dot(
            pre[HALO:, 2 * state + width :], pick_ref[...], preferred_element_type=jnp.float32
        )
        scale_ref[...] = scale[HALO:]
        dt_ref[...] = jax.nn.softplus(raw + dtb_ref[...])
        conv_ref[...] = conv_silu(wide, taps_ref, bias_ref, cores * span)

        def one_block(k, before):
            here = pl.ds(pl.multiple_of(k * span, span), span)
            dt = dt_ref[here, :]
            rise = dt * rate_ref[...]
            lower = lower_ref[...]
            cum = sum(
                jnp.dot(lower.astype(jnp.bfloat16), part, preferred_element_type=jnp.float32)
                for part in reversed(split(rise))
            )
            b = conv_ref[here, :state]
            c_conv = conv_ref[here, state : 2 * state]
            x = conv_ref[here, 2 * state :]
            y, st = block_terms(heads, b, c_conv, x, dt, cum, lower, skip_ref[...])
            y_ref[i, k] = y
            c_ref[i, k] = c_conv
            cum_ref[i, k, :, :heads] = cum
            cum_ref[i, k, :, heads:] = scale_ref[here, :]
            end = jnp.exp(-cum[span - 1 : span, :])
            first = k == 0
            decay = jnp.where(first, end, before * end)
            joined = jnp.where(first, 0.0, st_ref[i]) * spread_rows(end, heads) + st

            @pl.when(first)
            def _():
                st_ref[i] = joined

            @pl.when(jnp.logical_not(first))
            def _():
                joined_ref[...] = joined

            return decay

        decay = lax.fori_loop(0, cores, one_block, jnp.ones((1, heads), jnp.float32))
        for row, part in enumerate(split(decay)):
            tail_ref[row : row + 1, :heads] = part.astype(jnp.float32)
        for r, out in enumerate(pair_refs):
            first_row = share_start((place_ref[2] + r) % depth, inner, share)
            out[i, :share, :] = joined_ref[pl.ds(first_row, share), :].astype(jnp.bfloat16)
            out[i, share:, :] = tail_ref[...].astype(jnp.bfloat16)
        return carry

    lax.fori_loop(0, count, one_chunk, 0)


def scan_kernel(inner, place_ref, *refs):
    depth = (len(refs) - 2) // 2
    parts, outs, (held, enter) = refs[:depth], refs[depth:-2], refs[-2:]
    q = place_ref[1]
    z = place_ref[2]
    sections, share, state = outs[0].shape
    for r, part in enumerate(parts):
        held[(z + depth - r) % depth] = part[...]
    row = lax.broadcasted_iota(jnp.int32, (share, state), 0) + share_start(z, inner, share)
    lane = lax.broadcasted_iota(jnp.int32, (share, state), 1)

    def step(k, running):
        s = k // depth
        zz = k % depth
        m = place_ref[3 + (s ^ q)]
        enter[zz, m] = running.astype(jnp.bfloat16)
        tail = held[zz, m, share:, :].astype(jnp.float32)
        decay = tail[0:1, :] + tail[1:2, :] + tail[2:3, :]
        decay = jnp.sum(jnp.where(row // HEADDIM == lane, decay, 0.0), axis=1, keepdims=True)
        return running * decay + held[zz, m, :share, :].astype(jnp.float32)

    lax.fori_loop(0, sections * depth, step, jnp.zeros((share, state), jnp.float32), unroll=True)
    for d, out in enumerate(outs):
        out[...] = enter[(z + d) % depth]


def silu(wide, scale):
    gate = (wide * scale).astype(jnp.bfloat16).astype(jnp.float32)
    return gate * jax.nn.sigmoid(gate)


def silu_kernel(chunks, heads, place_ref, *refs):
    count = len(chunks)
    rows_mine, rows_other = refs[:count], refs[count : 2 * count]
    both_ref, cum_ref, out_ref, mat_ref, held, arrived, loaded = refs[2 * count :]
    cores, span, inner = out_ref.shape[1:]
    c = place_ref[0]
    _, _, shift = window(c, inner)

    def copies(i):
        return rows_copies(
            rows_mine[i], rows_other[i], held.at[i % 2], arrived.at[i % 2], c, 0
        )

    weights = window_copies(both_ref, (0, 0), mat_ref, c, inner, loaded)
    for copy in weights + copies(0):
        copy.start()
    for copy in weights:
        copy.wait()
    for i, m in enumerate(chunks):
        if i + 1 < count:
            for copy in copies(i + 1):
                copy.start()
        for copy in copies(i):
            copy.wait()
        wide = jnp.dot(held[i % 2], mat_ref[...], preferred_element_type=jnp.float32)
        wide = chosen(wide, c, inner, shift)
        for k in range(cores):
            out_ref[i, k] = silu(wide[k * span : (k + 1) * span], cum_ref[m, k, :, heads:])


def gate_kernel(heads, m, ready, place_ref, y_ref, c_ref, cum_ref, st_ref, *refs):
    if ready is None:
        rows_mine, rows_other, mat_ref, *refs, held, arrived = refs
    else:
        silu_ref, *refs = refs
    *parts, out_ref, enter = refs
    cores, span, inner = out_ref.shape
    c = place_ref[0]
    z = place_ref[2]
    depth = len(parts)
    share = parts[0].shape[1]
    _, _, shift = window(c, inner)
    copies = []
    if ready is None:
        copies = rows_copies(rows_mine, rows_other, held, arrived, c, 0)
    for copy in copies:
        copy.start()
    for d, part in enumerate(parts):
        enter[pl.ds(share_start((z + depth - d) % depth, inner, share), share), :] = part[m]
    end = spread_rows(jnp.exp(-cum_ref[m, 0, span - 1 : span, :heads]), heads)
    second = enter[...].astype(jnp.float32) * end + st_ref[m]
    totals = []
    for k, start in enumerate((enter[...], second.astype(jnp.bfloat16))):
        reached = lax.dot_general(
            c_ref[m, k], start, (((1,), (1,)), ((), ())), preferred_element_type=jnp.float32
        )
        totals.append(y_ref[m, k] + reached * spread(jnp.exp(-cum_ref[m, k, :, :heads]), heads))
    for copy in copies:
        copy.wait()
    if ready is None:
        wide = jnp.dot(held[...], mat_ref[...], preferred_element_type=jnp.float32)
        wide = chosen(wide, c, inner, shift)
    for k, total in enumerate(totals):
        if ready is None:
            gate = silu(wide[k * span : (k + 1) * span], cum_ref[m, k, :, heads:])
        else:
            gate = silu_ref[ready, k]
        out_ref[c ^ k] = (total * gate).astype(jnp.bfloat16)


def norm_kernel(masks, place_ref, *refs):
    gain_ref, out_ref = refs[-2:]
    pieces = refs[:-2]
    c = place_ref[0]
    q = place_ref[1]
    part = pieces[0].shape[-1]
    values = [r[...].astype(jnp.float32) for r in pieces]
    total = sum(jnp.sum(v * v, axis=-1, keepdims=True) for v in values)
    scale = lax.rsqrt(total / (part * len(pieces)) + EPS)
    values = [v * scale for v in values]
    cores = len(masks)
    for here in range(cores):
        for s in range(len(pieces) // cores):

            @pl.when((q == s) & (c == here))
            def _(here=here, s=s):
                for m in range(len(masks[0])):
                    for k in range(cores):
                        core = here ^ k
                        group = (s ^ masks[core][m]) * cores + core
                        first = group * part
                        out_ref[:, first : first + part] = (
                            values[m * cores + k] * gain_ref[:, first : first + part]
                        ).astype(jnp.bfloat16)


def per_device(
    tokens,
    pre_gain,
    w_z,
    w_x,
    w_bc,
    w_dt,
    conv_weight,
    conv_bias,
    dt_bias,
    a_log,
    d_skip,
    norm_gain,
):
    sections, depth, cores = (lax.axis_size(axis) for axis in ALL)
    q, z, c = (lax.axis_index(axis) for axis in ALL)
    span, width = tokens.shape
    state = w_bc.shape[1] // 2
    heads = a_log.shape[0] // (sections * cores)
    inner = heads * HEADDIM
    group = q * cores + c
    smem = pl.BlockSpec(memory_space=pltpu.SMEM)
    vmem = pl.BlockSpec(memory_space=pltpu.VMEM)
    masks = ((0, 2, 1, 3), (0, 1, 2, 3))
    order = [jnp.where(c == 0, masks[0].index(k), masks[1].index(k)) for k in range(sections)]
    place = jnp.stack([c, q, z] + order).astype(jnp.int32)

    hbm = pl.BlockSpec(memory_space=pltpu.HBM)

    def call(kernel, out_shape, *operands, scratch=(), scalars=False, far=(), near=(), load=0):
        operands = [
            pltpu.with_memory_space_constraint(v, pltpu.HBM if i in far else pltpu.VMEM)
            if i in far or i in near
            else v
            for i, v in enumerate(operands)
        ]
        return pl.pallas_call(
            kernel,
            out_shape=out_shape,
            in_specs=[
                smem if scalars and i == 0 else hbm if i in far else vmem
                for i in range(len(operands))
            ],
            scratch_shapes=list(scratch),
            compiler_params=params(),
            cost_estimate=pl.CostEstimate(
                flops=0, bytes_accessed=0, transcendentals=0
            ),
        )(*operands)

    height = w_x.shape[0]
    gain = lax.dynamic_slice_in_dim(pre_gain, (z * cores + c) * height, height, 0)[:, None]

    def quarter(matrix):
        return lax.dynamic_slice_in_dim(matrix, q * (cores * inner), cores * inner, 1)

    def gathered_rows(matrix):
        matrix = (matrix.astype(jnp.float32) * gain).astype(jnp.bfloat16)
        return lax.all_gather(matrix, ("zed", "core"), axis=0, tiled=True)

    steps = -(-w_dt.shape[1] // LANES) * LANES
    dt_columns = jnp.pad(w_dt, ((0, 0), (0, steps - w_dt.shape[1])))
    both_x = gathered_rows(jnp.concatenate([w_bc, quarter(w_x), dt_columns], 1))
    both_z = gathered_rows(quarter(w_z))

    first_hop = routed(tokens, (masks[0][1], masks[1][1]))
    second_hop = routed(tokens, (masks[0][2], masks[1][2]))
    halo = before_chip(tokens[span - HALO :])
    halos = [halo] + [routed(halo, (masks[0][m], None)) for m in range(1, sections)]
    first_hop, halos = lax.optimization_barrier((first_hop, halos))
    diagonal = routed(first_hop, (masks[0][2], masks[1][2]))
    rows_mine = [tokens, first_hop, second_hop, diagonal]
    halos = jnp.stack(halos)
    halos = [halos, swapped(halos, "core", 1)]

    first = group * heads
    (dt_bias, a_log, d_skip, conv_weight, conv_bias), _ = lax.optimization_barrier(
        ((dt_bias, a_log, d_skip, conv_weight, conv_bias), halos[0])
    )

    def mine(vector):
        return lax.dynamic_slice_in_dim(vector, first, heads, 0)[None, :]

    def channels(matrix):
        x_side = lax.dynamic_slice_in_dim(matrix, group * inner, inner, 1)
        return jnp.concatenate([matrix[:, -2 * state :], x_side], 1)

    dtb = mine(dt_bias)
    rate = jnp.exp(mine(a_log))
    skip = jnp.repeat(mine(d_skip), HEADDIM, axis=1)
    taps, bias = channels(conv_weight), channels(conv_bias[None, :])
    pick = (
        lax.broadcasted_iota(jnp.int32, (steps, heads), 0)
        == lax.broadcasted_iota(jnp.int32, (steps, heads), 1) + first
    ).astype(jnp.bfloat16)
    crossed = [swapped(v, "core", 1) for v in rows_mine]
    rows_other = [crossed[0], crossed[2], crossed[1], crossed[3]]
    share = share_of(inner, depth)
    view = window(0, inner)[1]
    n = sections
    y, c_conv, cum, st, *parts = call(
        functools.partial(
            chunk_kernel, heads, state, [(m, masks[0].index(masks[1][m])) for m in range(n)]
        ),
        (
            pltpu.VMEM((n, cores, span, inner), jnp.float32),
            pltpu.VMEM((n, cores, span, state), jnp.bfloat16),
            pltpu.VMEM((n, cores, span, heads + 1), jnp.float32),
            pltpu.VMEM((n, inner, state), jnp.float32),
        )
        + (jax.ShapeDtypeStruct((n, share + HALO, state), jnp.bfloat16),) * depth,
        place, *rows_mine, *rows_other, *halos, both_x, pick, taps, bias, dtb, rate, skip,
        scratch=[
            pltpu.VMEM((width, 2 * state + view + steps), jnp.bfloat16),
            pltpu.VMEM((2, HALO + cores * span, width), jnp.bfloat16),
            pltpu.VMEM((HALO + cores * span, 2 * state + inner), jnp.float32),
            pltpu.VMEM((span, span), jnp.float32),
            pltpu.VMEM((cores * span, 1), jnp.float32),
            pltpu.VMEM((cores * span, heads), jnp.float32),
            pltpu.VMEM((cores * span, 2 * state + inner), jnp.bfloat16),
            pltpu.VMEM((inner, state), jnp.float32),
            pltpu.VMEM((HALO, state), jnp.float32),
            pltpu.SemaphoreType.DMA((2, 1 + cores)),
            pltpu.SemaphoreType.DMA((3,)),
        ],
        scalars=True,
        far=range(1, 1 + 2 * n + 3),
        load=6 * n * cores * span * width * (2 * state + view + steps),
    )

    def along(values):
        return [values[0]] + [
            lax.ppermute(v, "zed", [(i, (i + r) % depth) for i in range(depth)])
            for r, v in enumerate(values)
            if r
        ]

    enters = call(
        functools.partial(scan_kernel, inner),
        (jax.ShapeDtypeStruct((n, share, state), jnp.bfloat16),) * depth,
        place,
        *along(parts),
        scratch=[
            pltpu.VMEM((depth, n, share + HALO, state), jnp.bfloat16),
            pltpu.VMEM((depth, n, share, state), jnp.bfloat16),
        ],
        scalars=True,
    )
    both_z, enters = lax.optimization_barrier((both_z, enters))
    enters = along(enters)

    early = (sections - 1,)
    silus, full_z = call(
        functools.partial(silu_kernel, early, heads),
        (
            pltpu.VMEM((len(early), cores, span, inner), jnp.float32),
            pltpu.VMEM((width, view), jnp.bfloat16),
        ),
        place,
        *[rows_mine[m] for m in early],
        *[rows_other[m] for m in early],
        both_z,
        cum,
        scratch=[
            pltpu.VMEM((2, cores * span, width), jnp.bfloat16),
            pltpu.SemaphoreType.DMA((2, cores)),
            pltpu.SemaphoreType.DMA((3,)),
        ],
        scalars=True,
        far=range(1, 2 + 2 * len(early)),
        near=(2 + 2 * len(early),),
        load=5 * len(early) * cores * span * width * view,
    )
    pieces = [None] * (sections * cores)
    sent = []
    for m in (3, 1, 2, 0):
        if m in early:
            extra, far = (silus,), ()
        else:
            extra, far = (rows_mine[m], rows_other[m], full_z), (5, 6)
        gated = call(
            functools.partial(gate_kernel, heads, m, early.index(m) if m in early else None),
            jax.ShapeDtypeStruct((cores, span, inner), jnp.bfloat16),
            place, y, c_conv, cum, st, *extra, *enters,
            scratch=[
                pltpu.VMEM((inner, state), jnp.bfloat16),
            ]
            + [
                pltpu.VMEM((cores * span, width), jnp.bfloat16),
                pltpu.SemaphoreType.DMA((cores,)),
            ]
            * (m not in early),
            scalars=True,
            far=far,
            near=(1, 2, 3, 4, 5 if m in early else 7),
            load=(1 if m in early else 5) * cores * span * width * view,
        )
        if m:
            before = gated
            gated = routed(gated, (masks[0][m], masks[1][m]))
        sent.append(gated)
    for m, gated in zip((3, 1, 2, 0), sent):
        if m:
            gated, before = lax.optimization_barrier((gated, before))
        pieces[m * cores] = gated[0]
        before = pieces[m * cores + 1] = swapped(gated[1], "core", 1)
    return call(
        functools.partial(norm_kernel, masks),
        jax.ShapeDtypeStruct((span, sections * cores * inner), jnp.bfloat16),
        place,
        *pieces,
        norm_gain[None, :],
        scalars=True,
    )


def solution(mesh):
    sections, fsdp = (mesh.shape[axis] for axis in ("sec", "fsdp"))
    split = Mesh(mesh.devices.reshape(sections, fsdp // 2, 2), ALL)
    rows = P(("zed", "core"), None)
    placed = (P(ALL, None), P(), rows, rows, rows, rows, P(), P(), P(), P(), P(), P())
    return jax.shard_map(
        per_device, mesh=split, in_specs=placed, out_specs=P(ALL, None), check_vma=False
    )
```

```python
import functools
import jax
import jax.numpy as jnp
from jax import lax
from jax.experimental import pallas as pl
from jax.experimental.pallas import tpu as pltpu
from jax.sharding import Mesh, PartitionSpec as P

HEADDIM = 64
EPS = 1e-05
HALO = 16
LANES = 128
VMEM_LIMIT = 22 * 1024 * 1024
ALL = ("sec", "zed", "core")


def params():
    return pltpu.CompilerParams(vmem_limit_bytes=VMEM_LIMIT)


def swapped(value, axis, mask):
    count = lax.axis_size(axis)
    return lax.ppermute(value, axis, [(i, i ^ mask) for i in range(count)])


def routed(value, masks):
    sections, depth, cores = (lax.axis_size(axis) for axis in ALL)
    pairs = []
    for s in range(sections):
        for z in range(depth):
            for c in range(cores):
                if masks[c] is None:
                    continue
                place = z * cores + c
                pairs.append(
                    (s * depth * cores + place, (s ^ masks[c]) * depth * cores + place)
                )
    return lax.ppermute(value, ALL, pairs)


def before_chip(tail):
    sections, depth, cores = (lax.axis_size(axis) for axis in ALL)
    chips = sections * depth
    return lax.ppermute(
        tail, ALL, [(i * cores + cores - 1, (i + 1) * cores) for i in range(chips - 1)]
    )


def split(value):
    high = value.astype(jnp.bfloat16)
    left = value - high.astype(jnp.float32)
    middle = left.astype(jnp.bfloat16)
    low = (left - middle.astype(jnp.float32)).astype(jnp.bfloat16)
    return high, middle, low


def spread(columns, heads):
    rows = columns.shape[0]
    return jnp.concatenate(
        [jnp.broadcast_to(columns[:, h : h + 1], (rows, HEADDIM)) for h in range(heads)],
        axis=1,
    )


def share_of(size, parts):
    return -(-size // (parts * HALO)) * HALO


def share_start(part, size, share):
    return pl.multiple_of(jnp.minimum(part * share, size - share), HALO)


def spread_rows(row, heads):
    return jnp.concatenate(
        [jnp.broadcast_to(row[:, h : h + 1], (HEADDIM, 1)) for h in range(heads)], axis=0
    )


def window(c, inner):
    shift = inner % LANES
    width = -(-(inner + shift) // LANES) * LANES
    return pl.multiple_of(c * (inner - shift), LANES), width, shift


def chosen(wide, c, inner, shift):
    return jnp.where(c == 0, wide[:, :inner], wide[:, shift : shift + inner])


def window_copies(both, columns, held, c, inner, sems):
    lead, rest = columns
    first, width, _ = window(c, inner)
    cuts = [(0, 0, lead), (lead + first, lead, width)]
    cuts.append((both.shape[1] - rest, lead + width, rest))
    copies = []
    for k, (source, target, size) in enumerate(cuts):
        if size:
            copies.append(
                pltpu.make_async_copy(
                    both.at[:, pl.ds(source, size)], held.at[:, pl.ds(target, size)], sems.at[k]
                )
            )
    return copies


def rows_copies(rows_mine, rows_other, held, sems, c, first):
    span = rows_mine.shape[0]
    copies = []
    for k, rows in enumerate((rows_mine, rows_other)):
        start = pl.multiple_of(first + (c ^ k) * span, HALO)
        copies.append(
            pltpu.make_async_copy(rows, held.at[pl.ds(start, span)], sems.at[k])
        )
    return copies


def conv_silu(wide, taps_ref, bias_ref, span):
    taps = taps_ref.shape[0]
    acc = bias_ref[...]
    for k in range(taps):
        acc = acc + taps_ref[k : k + 1, :] * wide[pl.ds(HALO - taps + 1 + k, span), :]
    return (acc * jax.nn.sigmoid(acc)).astype(jnp.bfloat16)


def block_terms(heads, b, c_conv, x, dt, cum, lower, skip):
    span = b.shape[0]
    cum_t = cum.T
    dt_t = dt.T
    inner_dots = lax.dot_general(
        c_conv, b, (((1,), (1,)), ((), ())), preferred_element_type=jnp.float32
    )
    inner_dots = inner_dots * lower
    half = span // 2
    parts = []
    for h in range(heads):
        x_head = x[:, h * HEADDIM : (h + 1) * HEADDIM]
        rows_of = []
        for low_row, high_row in ((0, half), (half, span)):
            gap = cum_t[h : h + 1, :high_row] - cum[low_row:high_row, h : h + 1]
            scores = (
                inner_dots[low_row:high_row, :high_row]
                * jnp.exp(jnp.minimum(gap, 0.0))
                * dt_t[h : h + 1, :high_row]
            )
            rows_of.append(
                jnp.dot(
                    scores.astype(jnp.bfloat16),
                    x_head[:high_row],
                    preferred_element_type=jnp.float32,
                )
            )
        parts.append(jnp.concatenate(rows_of, 0))
    x32 = x.astype(jnp.float32)
    y = jnp.concatenate(parts, axis=1) + skip * x32
    to_end = jnp.exp(cum - cum[span - 1 : span, :]) * dt
    weighted = (x32 * spread(to_end, heads)).astype(jnp.bfloat16)
    st = lax.dot_general(
        weighted, b, (((0,), (0,)), ((), ())), preferred_element_type=jnp.float32
    )
    return y, st


def chunk_kernel(heads, state, chunks, place_ref, *refs):
    count = len(chunks)
    rows_mine, rows_other = refs[:count], refs[count : 2 * count]
    (halo_mine, halo_other, source_ref, dt_mine, dt_other, pick_ref, taps_ref, bias_ref, dtb_ref, rate_ref, skip_ref,
     y_ref, c_ref, cum_ref, st_ref) = refs[2 * count : 2 * count + 15]
    pair_refs = refs[2 * count + 15 : -11]
    (mat_ref, held, wide, lower_ref, scale_ref, dt_ref, conv_ref, joined_ref, tail_ref, arrived,
     loaded) = refs[-11:]
    c = place_ref[0]
    cores, span = y_ref.shape[1:3]
    inner = heads * HEADDIM
    _, width, shift = window(c, inner)
    steps = mat_ref.shape[1] - width - 2 * state
    depth = len(pair_refs)
    share = share_of(inner, depth)

    def halo_copy(i, slot, core):
        source, m = ((halo_mine, chunks[i][0]), (halo_other, chunks[i][1]))[core]
        return pltpu.make_async_copy(source.at[m], held.at[slot, :HALO], arrived.at[slot, cores])

    def all_rows(i, slot):
        return rows_copies(
            rows_mine[i], rows_other[i], held.at[slot], arrived.at[slot], c, HALO
        )

    def start(i):
        for copy in all_rows(i, i % 2):
            copy.start()
        for core in range(cores):

            @pl.when(c == core)
            def _(core=core):
                halo_copy(i, i % 2, core).start()

    weights = window_copies(source_ref, (2 * state, 0), mat_ref, c, inner, loaded)
    for copy in weights:
        copy.start()
    start(0)
    height = mat_ref.shape[0] // (depth * cores)
    for k, ref in enumerate((dt_mine, dt_other)):
        for r in range(depth):
            turned = ref[r * HALO : (r + 1) * HALO, :].astype(jnp.float32).T[:height]
            turned = jnp.concatenate([turned, jnp.zeros((height, steps - HALO), jnp.float32)], 1)
            block = (place_ref[2] + depth - r) % depth * cores + (c ^ k)
            here = pl.ds(pl.multiple_of(block * height, HALO), height)
            mat_ref[here, 2 * state + width :] = turned.astype(jnp.bfloat16)
    tail_ref[...] = jnp.zeros_like(tail_ref)
    st_ref[...] = jnp.zeros_like(st_ref)
    row = lax.broadcasted_iota(jnp.int32, (span, span), 0)
    col = lax.broadcasted_iota(jnp.int32, (span, span), 1)
    lower_ref[...] = (row >= col).astype(jnp.float32)
    for copy in weights:
        copy.wait()

    def one_chunk(i, carry):
        for j in range(1, count):

            @pl.when(i + 1 == j)
            def _(j=j):
                start(j)

        slot = i % 2
        for copy in all_rows(0, slot):
            copy.wait()
        halo_copy(0, slot, 0).wait()
        rows = held[slot]
        values = rows.astype(jnp.float32)
        scale = lax.rsqrt(jnp.mean(values * values, axis=-1, keepdims=True) + EPS)
        total = jnp.dot(rows, mat_ref[...], preferred_element_type=jnp.float32)
        pre = (total * scale).astype(jnp.bfloat16)
        wide[:, : 2 * state] = pre[:, : 2 * state].astype(jnp.float32)
        window_part = pre[:, 2 * state : 2 * state + width].astype(jnp.float32)
        wide[:, 2 * state :] = chosen(window_part, c, inner, shift)
        raw = jnp.dot(
            pre[HALO:, 2 * state + width :], pick_ref[...], preferred_element_type=jnp.float32
        )
        scale_ref[...] = scale[HALO:]
        dt_ref[...] = jax.nn.softplus(raw + dtb_ref[...])
        conv_ref[...] = conv_silu(wide, taps_ref, bias_ref, cores * span)

        def one_block(k, before):
            here = pl.ds(pl.multiple_of(k * span, span), span)
            dt = dt_ref[here, :]
            rise = dt * rate_ref[...]
            lower = lower_ref[...]
            cum = sum(
                jnp.dot(lower.astype(jnp.bfloat16), part, preferred_element_type=jnp.float32)
                for part in reversed(split(rise))
            )
            b = conv_ref[here, :state]
            c_conv = conv_ref[here, state : 2 * state]
            x = conv_ref[here, 2 * state :]
            y, st = block_terms(heads, b, c_conv, x, dt, cum, lower, skip_ref[...])
            y_ref[i, k] = y.astype(jnp.bfloat16)
            c_ref[i, k] = c_conv
            cum_ref[i, k, :, :heads] = cum
            cum_ref[i, k, :, heads:] = scale_ref[here, :]
            end = jnp.exp(-cum[span - 1 : span, :])
            first = k == 0
            decay = jnp.where(first, end, before * end)
            joined = jnp.where(first, 0.0, st_ref[i]) * spread_rows(end, heads) + st

            @pl.when(first)
            def _():
                st_ref[i] = joined

            @pl.when(jnp.logical_not(first))
            def _():
                joined_ref[...] = joined

            return decay

        decay = lax.fori_loop(0, cores, one_block, jnp.ones((1, heads), jnp.float32))
        for row, part in enumerate(split(decay)):
            tail_ref[row : row + 1, :heads] = part.astype(jnp.float32)
        for r, out in enumerate(pair_refs):
            first_row = share_start((place_ref[2] + r) % depth, inner, share)
            out[i, :share, :] = joined_ref[pl.ds(first_row, share), :].astype(jnp.bfloat16)
            out[i, share:, :] = tail_ref[...].astype(jnp.bfloat16)
        return carry

    lax.fori_loop(0, count, one_chunk, 0)


def scan_kernel(inner, place_ref, *refs):
    depth = (len(refs) - 3) // 2
    parts, outs, (held, enter, sent) = refs[:depth], refs[depth:-3], refs[-3:]
    q = place_ref[1]
    z = place_ref[2]
    sections, share, state = outs[0].shape
    for r, part in enumerate(parts):
        held[(z + depth - r) % depth] = part[...]
    row = lax.broadcasted_iota(jnp.int32, (share, state), 0) + share_start(z, inner, share)
    lane = lax.broadcasted_iota(jnp.int32, (share, state), 1)

    def step(k, running):
        s = k // depth
        zz = k % depth
        m = place_ref[3 + (s ^ q)]
        enter[zz, m] = running.astype(jnp.bfloat16)
        tail = held[zz, m, share:, :].astype(jnp.float32)
        decay = tail[0:1, :] + tail[1:2, :] + tail[2:3, :]
        decay = jnp.sum(jnp.where(row // HEADDIM == lane, decay, 0.0), axis=1, keepdims=True)
        return running * decay + held[zz, m, :share, :].astype(jnp.float32)

    lax.fori_loop(0, sections * depth, step, jnp.zeros((share, state), jnp.float32), unroll=True)
    copies = [
        pltpu.make_async_copy(enter.at[(z + d) % depth], out, sent.at[d])
        for d, out in enumerate(outs)
    ]
    for copy in copies:
        copy.start()
    for copy in copies:
        copy.wait()


def silu(wide, scale):
    gate = (wide * scale).astype(jnp.bfloat16).astype(jnp.float32)
    return gate * jax.nn.sigmoid(gate)


def silu_kernel(chunks, heads, place_ref, *refs):
    count = len(chunks)
    rows_mine, rows_other = refs[:count], refs[count : 2 * count]
    both_ref, cum_ref, out_ref, mat_ref, held, arrived, loaded = refs[2 * count :]
    cores, span, inner = out_ref.shape[1:]
    c = place_ref[0]
    _, _, shift = window(c, inner)

    def copies(i):
        return rows_copies(
            rows_mine[i], rows_other[i], held.at[i % 2], arrived.at[i % 2], c, 0
        )

    weights = window_copies(both_ref, (0, 0), mat_ref, c, inner, loaded)
    for copy in weights + copies(0):
        copy.start()
    for copy in weights:
        copy.wait()
    for i, m in enumerate(chunks):
        if i + 1 < count:
            for copy in copies(i + 1):
                copy.start()
        for copy in copies(i):
            copy.wait()
        wide = jnp.dot(held[i % 2], mat_ref[...], preferred_element_type=jnp.float32)
        wide = chosen(wide, c, inner, shift)
        for k in range(cores):
            out_ref[i, k] = silu(wide[k * span : (k + 1) * span], cum_ref[m, k, :, heads:])


def gate_kernel(heads, m, ready, place_ref, y_ref, c_ref, cum_ref, st_ref, *refs):
    if ready is None:
        rows_mine, rows_other, mat_ref, *parts, out_ref, enter = refs
    else:
        silu_ref, *parts, out_ref, enter = refs
    cores, span, inner = out_ref.shape
    c = place_ref[0]
    z = place_ref[2]
    depth = len(parts)
    share = parts[0].shape[1]
    _, _, shift = window(c, inner)
    for d, part in enumerate(parts):
        enter[pl.ds(share_start((z + depth - d) % depth, inner, share), share), :] = part[m]
    end = spread_rows(jnp.exp(-cum_ref[m, 0, span - 1 : span, :heads]), heads)
    entering = enter[...].astype(jnp.float32)
    second = entering * end + st_ref[m]
    for k in range(cores):
        block = c ^ k
        start = jnp.where(block == 0, entering, second).astype(jnp.bfloat16)
        cum = cum_ref[m, block]
        reached = lax.dot_general(
            c_ref[m, block], start, (((1,), (1,)), ((), ())), preferred_element_type=jnp.float32
        )
        total = y_ref[m, block].astype(jnp.float32) + reached * spread(jnp.exp(-cum[:, :heads]), heads)
        if ready is None:
            rows = (rows_mine, rows_other)[k]
            wide = jnp.dot(rows[...], mat_ref[...], preferred_element_type=jnp.float32)
            gate = silu(chosen(wide, c, inner, shift), cum[:, heads:])
        else:
            gate = silu_ref[ready, block]
        out_ref[k] = (total * gate).astype(jnp.bfloat16)


def norm_kernel(masks, place_ref, *refs):
    *pieces, gain_ref, out_ref, scale_ref = refs
    c = place_ref[0]
    q = place_ref[1]
    part = pieces[0].shape[-1]
    total = 0.0
    for r in pieces:
        value = r[...].astype(jnp.float32)
        total = total + jnp.sum(value * value, axis=-1, keepdims=True)
    scale_ref[...] = lax.rsqrt(total / (part * len(pieces)) + EPS)
    cores = len(masks)
    for here in range(cores):
        for s in range(len(pieces) // cores):

            @pl.when((q == s) & (c == here))
            def _(here=here, s=s):
                order = {}
                for m in range(len(masks[0])):
                    for k in range(cores):
                        core = here ^ k
                        order[(s ^ masks[core][m]) * cores + core] = pieces[m * cores + k]
                for group in range(0, len(pieces), cores):
                    pair = [order[group + k][...] for k in range(cores)]
                    value = jnp.concatenate(pair, 1).astype(jnp.float32)
                    first, last = group * part, (group + cores) * part
                    out_ref[:, first:last] = (
                        value * scale_ref[...] * gain_ref[:, first:last]
                    ).astype(jnp.bfloat16)


def per_device(
    tokens,
    pre_gain,
    w_z,
    w_x,
    w_bc,
    w_dt,
    conv_weight,
    conv_bias,
    dt_bias,
    a_log,
    d_skip,
    norm_gain,
):
    sections, depth, cores = (lax.axis_size(axis) for axis in ALL)
    q, z, c = (lax.axis_index(axis) for axis in ALL)
    span, width = tokens.shape
    state = w_bc.shape[1] // 2
    heads = a_log.shape[0] // (sections * cores)
    inner = heads * HEADDIM
    group = q * cores + c
    smem = pl.BlockSpec(memory_space=pltpu.SMEM)
    vmem = pl.BlockSpec(memory_space=pltpu.VMEM)
    masks = ((0, 2, 1, 3), (0, 1, 2, 3))
    order = [jnp.where(c == 0, masks[0].index(k), masks[1].index(k)) for k in range(sections)]
    place = jnp.stack([c, q, z] + order).astype(jnp.int32)

    hbm = pl.BlockSpec(memory_space=pltpu.HBM)

    def call(kernel, out_shape, *operands, scratch=(), scalars=False, far=(), near=(), load=0):
        operands = [
            pltpu.with_memory_space_constraint(v, pltpu.HBM if i in far else pltpu.VMEM)
            if i in far or i in near
            else v
            for i, v in enumerate(operands)
        ]
        return pl.pallas_call(
            kernel,
            out_shape=out_shape,
            in_specs=[
                smem if scalars and i == 0 else hbm if i in far else vmem
                for i in range(len(operands))
            ],
            scratch_shapes=list(scratch),
            compiler_params=params(),
            cost_estimate=pl.CostEstimate(
                flops=0, bytes_accessed=0, transcendentals=0
            ),
        )(*operands)

    def along(values):
        return [values[0]] + [
            lax.ppermute(v, "zed", [(i, (i + r) % depth) for i in range(depth)])
            for r, v in enumerate(values)
            if r
        ]

    height = w_x.shape[0]
    gain = lax.dynamic_slice_in_dim(pre_gain, (z * cores + c) * height, height, 0)[:, None]

    def quarter(matrix):
        return lax.dynamic_slice_in_dim(matrix, q * (cores * inner), cores * inner, 1)

    def gathered_rows(matrix):
        matrix = (matrix.astype(jnp.float32) * gain).astype(jnp.bfloat16)
        return lax.all_gather(matrix, ("zed", "core"), axis=0, tiled=True)

    steps = LANES
    both_x = gathered_rows(jnp.concatenate([w_bc, quarter(w_x)], 1))
    both_z = gathered_rows(quarter(w_z))

    first_hop = routed(tokens, (masks[0][1], masks[1][1]))
    second_hop = routed(tokens, (masks[0][2], masks[1][2]))
    halo = before_chip(tokens[span - HALO :])
    halos = [halo] + [routed(halo, (masks[0][m], None)) for m in range(1, sections)]
    dt_weights, _ = lax.optimization_barrier((w_dt, halo))
    dt_weights = lax.dynamic_slice_in_dim(dt_weights, q * (cores * heads), cores * heads, 1)
    dt_weights = (dt_weights.astype(jnp.float32) * gain).astype(jnp.bfloat16).T
    dt_weights = jnp.pad(
        dt_weights, ((0, -dt_weights.shape[0] % HALO), (0, -dt_weights.shape[1] % LANES))
    )
    dt_weights = jnp.concatenate(along([dt_weights] * depth), 0)
    first_hop, halos, dt_weights = lax.optimization_barrier((first_hop, halos, dt_weights))
    dt_weights = [dt_weights, swapped(dt_weights, "core", 1)]


    diagonal = routed(first_hop, (masks[0][2], masks[1][2]))
    rows_mine = [tokens, first_hop, second_hop, diagonal]
    halos = jnp.stack(halos)
    halos = [halos, swapped(halos, "core", 1)]

    first = group * heads
    (dt_bias, a_log, d_skip, conv_weight, conv_bias), _ = lax.optimization_barrier(
        ((dt_bias, a_log, d_skip, conv_weight, conv_bias), halos[0])
    )

    def mine(vector):
        return lax.dynamic_slice_in_dim(vector, first, heads, 0)[None, :]

    def channels(matrix):
        x_side = lax.dynamic_slice_in_dim(matrix, group * inner, inner, 1)
        return jnp.concatenate([matrix[:, -2 * state :], x_side], 1)

    dtb = mine(dt_bias)
    rate = jnp.exp(mine(a_log))
    skip = jnp.repeat(mine(d_skip), HEADDIM, axis=1)
    taps, bias = channels(conv_weight), channels(conv_bias[None, :])
    pick = (
        lax.broadcasted_iota(jnp.int32, (steps, heads), 0)
        == lax.broadcasted_iota(jnp.int32, (steps, heads), 1) + c * heads
    ).astype(jnp.bfloat16)
    crossed = [swapped(v, "core", 1) for v in rows_mine]
    rows_other = [crossed[0], crossed[2], crossed[1], crossed[3]]
    share = share_of(inner, depth)
    view = window(0, inner)[1]
    n = sections
    y, c_conv, cum, st, *parts = call(
        functools.partial(
            chunk_kernel, heads, state, [(m, masks[0].index(masks[1][m])) for m in range(n)]
        ),
        (
            pltpu.VMEM((n, cores, span, inner), jnp.bfloat16),
            pltpu.VMEM((n, cores, span, state), jnp.bfloat16),
            pltpu.VMEM((n, cores, span, heads + 1), jnp.float32),
            pltpu.VMEM((n, inner, state), jnp.float32),
        )
        + (jax.ShapeDtypeStruct((n, share + HALO, state), jnp.bfloat16),) * depth,
        place, *rows_mine, *rows_other, *halos, both_x, *dt_weights, pick, taps, bias, dtb, rate, skip,
        scratch=[
            pltpu.VMEM((width, 2 * state + view + steps), jnp.bfloat16),
            pltpu.VMEM((2, HALO + cores * span, width), jnp.bfloat16),
            pltpu.VMEM((HALO + cores * span, 2 * state + inner), jnp.float32),
            pltpu.VMEM((span, span), jnp.float32),
            pltpu.VMEM((cores * span, 1), jnp.float32),
            pltpu.VMEM((cores * span, heads), jnp.float32),
            pltpu.VMEM((cores * span, 2 * state + inner), jnp.bfloat16),
            pltpu.VMEM((inner, state), jnp.float32),
            pltpu.VMEM((HALO, state), jnp.float32),
            pltpu.SemaphoreType.DMA((2, 1 + cores)),
            pltpu.SemaphoreType.DMA((3,)),
        ],
        scalars=True,
        far=range(1, 1 + 2 * n + 3),
        load=6 * n * cores * span * width * (2 * state + view + steps),
    )

    enters = call(
        functools.partial(scan_kernel, inner),
        (pltpu.HBM((n, share, state), jnp.bfloat16),) * depth,
        place,
        *along(parts),
        scratch=[
            pltpu.VMEM((depth, n, share + HALO, state), jnp.bfloat16),
            pltpu.VMEM((depth, n, share, state), jnp.bfloat16),
            pltpu.SemaphoreType.DMA((depth,)),
        ],
        scalars=True,
    )
    both_z, enters = lax.optimization_barrier((both_z, enters))
    enters = along(enters)

    early = (sections - 1,)
    silus, full_z = call(
        functools.partial(silu_kernel, early, heads),
        (
            pltpu.VMEM((len(early), cores, span, inner), jnp.float32),
            pltpu.VMEM((width, view), jnp.bfloat16),
        ),
        place,
        *[rows_mine[m] for m in early],
        *[rows_other[m] for m in early],
        both_z,
        cum,
        scratch=[
            pltpu.VMEM((2, cores * span, width), jnp.bfloat16),
            pltpu.SemaphoreType.DMA((2, cores)),
            pltpu.SemaphoreType.DMA((3,)),
        ],
        scalars=True,
        far=range(1, 2 + 2 * len(early)),
        near=(2 + 2 * len(early),),
        load=5 * len(early) * cores * span * width * view,
    )
    pieces = [None] * (sections * cores)
    sent = []
    for m in (3, 1, 2, 0):
        if m in early:
            extra, far = (silus,), ()
        else:
            extra, far = (rows_mine[m], rows_other[m], full_z), ()
        gated = call(
            functools.partial(gate_kernel, heads, m, early.index(m) if m in early else None),
            jax.ShapeDtypeStruct((cores, span, inner), jnp.bfloat16),
            place, y, c_conv, cum, st, *extra, *enters,
            scratch=[pltpu.VMEM((inner, state), jnp.bfloat16)],
            scalars=True,
            far=far,
            near=(1, 2, 3, 4, *((5,) if m in early else (5, 6, 7))),
            load=(1 if m in early else 5) * cores * span * width * view,
        )
        if m:
            before = gated
            gated = routed(gated, (masks[0][m], masks[1][m]))
        sent.append(gated)
    for m, gated in zip((3, 1, 2, 0), sent):
        if m:
            gated, before = lax.optimization_barrier((gated, before))
        pieces[m * cores] = gated[0]
        before = pieces[m * cores + 1] = swapped(gated[1], "core", 1)
    return call(
        functools.partial(norm_kernel, masks),
        jax.ShapeDtypeStruct((span, sections * cores * inner), jnp.bfloat16),
        place,
        *pieces,
        norm_gain[None, :],
        scratch=[pltpu.VMEM((span, 1), jnp.float32)],
        scalars=True,
    )


def solution(mesh):
    sections, fsdp = (mesh.shape[axis] for axis in ("sec", "fsdp"))
    split = Mesh(mesh.devices.reshape(sections, fsdp // 2, 2), ALL)
    rows = P(("zed", "core"), None)
    placed = (P(ALL, None), P(), rows, rows, rows, rows, P(), P(), P(), P(), P(), P())
    return jax.shard_map(
        per_device, mesh=split, in_specs=placed, out_specs=P(ALL, None), check_vma=False
    )
```
